32 devices in a mesh: frame: 4 (over x, core), rows: 8 (over z, y).
Axes of the slice: x: 2, y: 2, z: 4, core: 2. Of those that a mesh axis runs over, the one named last changes fastest.
Arguments:
- video: bfloat16 [2, 4, 8, 480, 256], P(None, 'frame', 'rows'), may hold values from -6 to 6
- stereo_qk: bfloat16 [256, 512], replicated, may hold values from -8 to 8
- stereo_v: bfloat16 [256, 256], replicated, may hold values from -0.375 to 0.375
- stereo_out: bfloat16 [256, 256], replicated, may hold values from -0.375 to 0.375
- temporal_qk: bfloat16 [256, 512], replicated, may hold values from -8 to 8
- temporal_v: bfloat16 [256, 256], replicated, may hold values from -0.375 to 0.375
- temporal_out: bfloat16 [256, 256], replicated, may hold values from -0.375 to 0.375
- mlp_up: bfloat16 [256, 1024], replicated, may hold values from -0.375 to 0.375
- mix_kernel: bfloat16 [3, 3, 1024], replicated, may hold values from -2 to 2
- mlp_down: bfloat16 [1024, 256], replicated, may hold values from -0.1875 to 0.1875
Outputs:
- block_output: bfloat16 [2, 4, 8, 480, 256], P(None, 'frame', 'rows')
The draws below stay inside these ranges and needn't reach their ends.
All inputs are finite; a program needn't handle non-finite values.
Results may differ from the reference program's by a relative error of at most 0.013.
Values may be sent and summed in bfloat16 or wider, within the bound.
No kernel may reach another device: no remote copies, remote signals or barrier semaphores. Data moves between devices by JAX's collectives and lax.ppermute only.
A program may use at most 64 MiB of HBM per device.

```python
import jax
import jax.numpy as jnp
from jax import lax

HEADS = 8
HEAD_DIM = 32
C = 256
FF = 1024
W = 480
FRAMES = 4
HEIGHT = 8


def draw_video(key, part):
    first_key = jax.random.fold_in(key, 0)
    base_draw = jax.random.normal(first_key, (2, FRAMES, HEIGHT, W, C), jnp.float32)
    result = base_draw
    return jnp.clip(result, -6.0, 6.0).astype(jnp.bfloat16)


def query_key_draw(base_key, salt):
    salted = jax.random.fold_in(base_key, salt)
    first_key, second_key = jax.random.split(salted, 2)
    query_part = jax.random.normal(first_key, (C, C), jnp.float32) * C ** (-0.5)
    noise_part = jax.random.normal(second_key, (C, C), jnp.float32) * C ** (-0.5)
    key_part = noise_part
    return jnp.clip(jnp.concatenate([query_part, key_part], axis=1), -8.0, 8.0)


def draw_stereo_qk(key, part):
    return query_key_draw(key, 11).astype(jnp.bfloat16)


def draw_temporal_qk(key, part):
    return query_key_draw(key, 23).astype(jnp.bfloat16)


def bell_draw(rng, extent, width, bound, dtype=jnp.bfloat16):
    values = jax.random.normal(rng, extent, jnp.float32) * width
    return jnp.minimum(jnp.maximum(values, -bound), bound).astype(dtype)


def setup_inputs(seed: int = 0) -> dict:
    keys = jax.random.split(jax.random.key(seed), 11)
    video = draw_video(jax.random.fold_in(keys[10], 71), 0)
    stereo_qk = draw_stereo_qk(jax.random.fold_in(keys[10], 71), 0)
    stereo_v = bell_draw(keys[2], (C, C), C ** -0.5, 0.375)
    stereo_out = bell_draw(keys[3], (C, C), C ** -0.5, 0.375)
    temporal_qk = draw_temporal_qk(jax.random.fold_in(keys[10], 71), 0)
    temporal_v = bell_draw(keys[5], (C, C), C ** -0.5, 0.375)
    temporal_out = bell_draw(keys[6], (C, C), C ** -0.5, 0.375)
    mlp_up = bell_draw(keys[7], (C, FF), C ** -0.5, 0.375)
    mix_kernel = bell_draw(keys[8], (3, 3, FF), 9 ** -0.5, 2.0)
    mlp_down = bell_draw(keys[9], (FF, C), FF ** -0.5, 0.1875)
    return {"video": video, "stereo_qk": stereo_qk, "stereo_v": stereo_v, "stereo_out": stereo_out, "temporal_qk": temporal_qk, "temporal_v": temporal_v, "temporal_out": temporal_out, "mlp_up": mlp_up, "mix_kernel": mix_kernel, "mlp_down": mlp_down}


def layer_norm(values_in):
    widened = values_in.astype(jnp.float32)
    centred = widened - lax.optimization_barrier(jnp.mean(widened, axis=-1, keepdims=True))
    variance = lax.optimization_barrier(jnp.mean(centred * centred, axis=-1, keepdims=True))
    return (centred * lax.rsqrt(variance + 1e-05)).astype(jnp.bfloat16)

def stereo_row(image_row, stereo_qk, stereo_v, stereo_out):
    normed = layer_norm(image_row).reshape(2 * W, C)
    paired = jnp.dot(normed, stereo_qk, preferred_element_type=jnp.float32).astype(jnp.bfloat16).reshape(2, W, 2 * C)
    value_rows = jnp.dot(normed, stereo_v, preferred_element_type=jnp.float32).astype(jnp.bfloat16).reshape(2, W, HEADS, HEAD_DIM)
    query_rows = paired[:, :, :C].reshape(2, W, HEADS, HEAD_DIM)
    keys_other = paired[::-1, :, C:].reshape(2, W, HEADS, HEAD_DIM)
    values_other = value_rows[::-1]
    score_scale = HEAD_DIM ** (-0.5)
    group_size = max(HEADS // 2, 1)
    results = []
    for offset in range(0, HEADS, group_size):
        scores = jnp.einsum('vqhd,vkhd->vhqk', query_rows[:, :, offset:offset + group_size].astype(jnp.float32), keys_other[:, :, offset:offset + group_size].astype(jnp.float32)) * score_scale
        weights = jax.nn.softmax(scores, axis=-1).astype(jnp.bfloat16)
        results.append(jnp.einsum('vhqk,vkhd->vqhd', weights.astype(jnp.float32), values_other[:, :, offset:offset + group_size].astype(jnp.float32)).astype(jnp.bfloat16))
    attended = jnp.concatenate(results, axis=2).reshape(2 * W, C)
    update = jnp.dot(attended, stereo_out, preferred_element_type=jnp.float32)
    return (image_row.astype(jnp.float32) + update.reshape(image_row.shape)).astype(jnp.bfloat16)

def temporal_attend(query_rows, key_rows, value_rows):
    shaped = query_rows.shape[:-1] + (HEADS, HEAD_DIM)
    scores = jnp.einsum('vfphd,vgphd->vphfg', query_rows.reshape(shaped).astype(jnp.float32), key_rows.reshape(shaped).astype(jnp.float32)) * HEAD_DIM ** (-0.5)
    weights = jax.nn.softmax(scores, axis=-1).astype(jnp.bfloat16)
    mixed_out = jnp.einsum('vphfg,vgphd->vfphd', weights.astype(jnp.float32), value_rows.reshape(shaped).astype(jnp.float32)).astype(jnp.bfloat16)
    return mixed_out.reshape(query_rows.shape)

def temporal_row(image_band, temporal_qk, temporal_v, temporal_out):
    normed = layer_norm(image_band).reshape(-1, C)
    paired = jnp.dot(normed, temporal_qk, preferred_element_type=jnp.float32).astype(jnp.bfloat16).reshape(2, FRAMES, W, 2 * C)
    value_rows = jnp.dot(normed, temporal_v, preferred_element_type=jnp.float32).astype(jnp.bfloat16).reshape(2, FRAMES, W, C)
    attended = temporal_attend(paired[..., :C], paired[..., C:], value_rows)
    update = jnp.dot(attended.reshape(-1, C), temporal_out, preferred_element_type=jnp.float32)
    return (image_band.astype(jnp.float32) + update.reshape(image_band.shape)).astype(jnp.bfloat16)

def expand_hidden(normed, mlp_up):
    pieces_out = []
    for view_index in range(normed.shape[0]):
        flat_rows = normed[view_index].reshape(-1, normed.shape[-1])
        product = jnp.dot(flat_rows, mlp_up, preferred_element_type=jnp.float32)
        pieces_out.append(jax.nn.gelu(product).astype(jnp.bfloat16).reshape(normed.shape[1:-1] + (mlp_up.shape[1],)))
    return jnp.stack(pieces_out)

def depthwise(padded, mix_kernel):
    rows_out = padded.shape[-3] - 2
    cols_out = padded.shape[-2]
    widened = jnp.pad(padded, [(0, 0)] * (padded.ndim - 2) + [(1, 1), (0, 0)])
    running = jnp.zeros(padded.shape[:-3] + (rows_out, cols_out, padded.shape[-1]), jnp.float32)
    for tap_row in range(3):
        for tap_col in range(3):
            window = widened[..., tap_row:tap_row + rows_out, tap_col:tap_col + cols_out, :]
            running = running + window.astype(jnp.float32) * mix_kernel[tap_row, tap_col].astype(jnp.float32)
    return running.astype(jnp.bfloat16)

def mlp_frame(frame_in, mlp_up, mix_kernel, mlp_down):
    normed = layer_norm(frame_in)
    hidden = expand_hidden(normed, mlp_up)
    padded = jnp.pad(hidden, ((0, 0), (1, 1), (0, 0), (0, 0)))
    mixed_out = depthwise(padded, mix_kernel)
    down_proj = jnp.dot(mixed_out.reshape(-1, FF), mlp_down, preferred_element_type=jnp.float32)
    return (frame_in.astype(jnp.float32) + down_proj.reshape(frame_in.shape)).astype(jnp.bfloat16)

def reference(video, stereo_qk, stereo_v, stereo_out, temporal_qk, temporal_v, temporal_out, mlp_up, mix_kernel, mlp_down):
    stereo_lines = jnp.transpose(video, (1, 2, 0, 3, 4)).reshape(FRAMES * HEIGHT, 2, W, C)
    after_lines = lax.map(lambda image_row: stereo_row(image_row, stereo_qk, stereo_v, stereo_out), stereo_lines)
    first_section = jnp.transpose(after_lines.reshape(FRAMES, HEIGHT, 2, W, C), (2, 0, 1, 3, 4))
    bands = jnp.transpose(first_section, (2, 0, 1, 3, 4))
    second_bands = lax.map(lambda image_band: temporal_row(image_band, temporal_qk, temporal_v, temporal_out), bands)
    second_section = jnp.transpose(second_bands, (1, 2, 0, 3, 4))
    frames_first = jnp.transpose(second_section, (1, 0, 2, 3, 4))
    outputs = lax.map(lambda frame_in: mlp_frame(frame_in, mlp_up, mix_kernel, mlp_down), frames_first)
    return jnp.transpose(outputs, (1, 0, 2, 3, 4))
```

```python
import functools

import jax
import jax.numpy as jnp
from jax import lax
from jax.experimental import pallas as pl
from jax.experimental.pallas import tpu as pltpu
from jax.sharding import PartitionSpec as P

HEADS = 8
HEAD_DIM = 32
SCALE_LOG2 = HEAD_DIM ** (-0.5) * 1.4426950408889634
VMEM_LIMIT = 40 * 1024 * 1024


def round_up(value, unit):
    return (value + unit - 1) // unit * unit


def layer_norm(widened):
    centred = widened - jnp.mean(widened, axis=-1, keepdims=True)
    variance = jnp.mean(centred * centred, axis=-1, keepdims=True)
    return (centred * lax.rsqrt(variance + 1e-05)).astype(jnp.bfloat16)


def dot_dims(lhs, rhs, lhs_dim, rhs_dim):
    return lax.dot_general(
        lhs, rhs, (((lhs_dim,), (rhs_dim,)), ((), ())), preferred_element_type=jnp.float32
    )


def stereo_kernel(left, cols, window, query_ref, other_ref, qk_ref, v_ref, out_ref, windows_ref):
    width, channels = query_ref.shape[-2:]
    rows = query_ref[...].reshape(width, channels).astype(jnp.float32)
    normed = layer_norm(rows)
    normed_other = layer_norm(other_ref[...].reshape(width, channels).astype(jnp.float32))
    queries = dot_dims(normed, qk_ref[:, :channels], 1, 0).astype(jnp.bfloat16)
    keys = dot_dims(normed_other, qk_ref[:, channels:], 1, 0).astype(jnp.bfloat16)
    values_t = dot_dims(v_ref[...], normed_other, 0, 1).astype(jnp.bfloat16)
    lane_head = lax.broadcasted_iota(jnp.int32, (width, 128), 1) // HEAD_DIM
    per_group = 128 // HEAD_DIM
    attended = []
    for head in range(HEADS):
        lanes = slice(head // per_group * 128, head // per_group * 128 + 128)
        keys_head = jnp.where(
            lane_head == head % per_group, keys[:, lanes], jnp.zeros((), jnp.bfloat16)
        )
        scores_t = dot_dims(keys_head, queries[:, lanes], 1, 1)
        top = jnp.max(scores_t, axis=0, keepdims=True)
        weights_t = jnp.exp2((scores_t - top) * SCALE_LOG2)
        total = jnp.sum(weights_t, axis=0, keepdims=True)
        mixed = dot_dims(
            values_t[head * HEAD_DIM : (head + 1) * HEAD_DIM], weights_t.astype(jnp.bfloat16), 1, 0
        )
        attended.append((mixed / total).astype(jnp.bfloat16))
    update = dot_dims(jnp.concatenate(attended, axis=0), out_ref[...], 0, 0)
    section = rows + update
    owners = width // cols
    tail = round_up((owners - 1) * cols + window, 8) - width
    padded = jnp.concatenate([section, jnp.zeros((tail, channels), jnp.float32)], axis=0)
    padded = pltpu.roll(padded, left, 0)
    for owner in range(owners):
        windows_ref[0, owner] = padded[owner * cols : owner * cols + window].astype(jnp.bfloat16)


def stereo(video, first, count, owners, left, window, stereo_qk, stereo_v, stereo_out):
    width, channels = video.shape[-2:]
    row_block = (1, 1, 1, width, channels)
    whole = lambda array: pl.BlockSpec(array.shape, lambda v: (0,) * array.ndim)
    return pl.pallas_call(
        functools.partial(stereo_kernel, left, width // owners, window),
        grid=(count,),
        in_specs=[
            pl.BlockSpec(row_block, lambda v: (first + v, 0, 0, 0, 0)),
            pl.BlockSpec(row_block, lambda v: (1 - first - v, 0, 0, 0, 0)),
            whole(stereo_qk),
            whole(stereo_v),
            whole(stereo_out),
        ],
        out_specs=pl.BlockSpec((1, owners, window, channels), lambda v: (v, 0, 0, 0)),
        out_shape=jax.ShapeDtypeStruct((count, owners, window, channels), jnp.bfloat16),
        compiler_params=pltpu.CompilerParams(vmem_limit_bytes=VMEM_LIMIT),
        cost_estimate=pl.CostEstimate(
            flops=count * 1_200_000_000, bytes_accessed=2_000_000, transcendentals=count * 2_000_000
        ),
        name="stereo",
    )(video, video, stereo_qk, stereo_v, stereo_out)


def head_sum(product):
    channels, width = product.shape
    return jnp.sum(product.reshape(HEADS, HEAD_DIM, width), axis=1, keepdims=True)


def temporal_kernel(side_ref, own_ref, other_ref, qk_ref, v_ref, out_ref, section_ref):
    _, _, frames, window, channels = own_ref.shape
    side = side_ref[0]
    for slot in range(2):
        rows = own_ref[0, slot].reshape(frames * window, channels).astype(jnp.float32)
        rows_other = other_ref[0, slot].reshape(frames * window, channels).astype(jnp.float32)
        normed = layer_norm(rows)
        normed_all = jnp.concatenate([normed, layer_norm(rows_other)], axis=0)
        queries = dot_dims(qk_ref[:, :channels], normed, 0, 1).astype(jnp.bfloat16)
        keys = dot_dims(qk_ref[:, channels:], normed_all, 0, 1).astype(jnp.bfloat16)
        values = dot_dims(v_ref[...], normed_all, 0, 1).astype(jnp.bfloat16)
        attended = []
        for frame in range(frames):
            query = queries[:, frame * window : (frame + 1) * window].astype(jnp.float32)
            scores = [
                head_sum(
                    query * keys[:, other * window : (other + 1) * window].astype(jnp.float32)
                )
                for other in range(2 * frames)
            ]
            top = functools.reduce(jnp.maximum, scores)
            weights = [jnp.exp2((score - top) * SCALE_LOG2) for score in scores]
            inverse = 1.0 / functools.reduce(jnp.add, weights)
            mixed = jnp.zeros((HEADS, HEAD_DIM, window), jnp.float32)
            for other in range(2 * frames):
                value = values[:, other * window : (other + 1) * window].astype(jnp.float32)
                mixed = mixed + value.reshape(HEADS, HEAD_DIM, window) * (
                    weights[other] * inverse
                )
            attended.append(mixed.reshape(channels, window).astype(jnp.bfloat16))
        update = dot_dims(jnp.concatenate(attended, axis=1), out_ref[...], 0, 0)
        section = (rows + update).astype(jnp.bfloat16)
        section_ref[0, side ^ slot] = section.reshape(frames, window, channels)


def temporal(side, own, other, temporal_qk, temporal_v, temporal_out):
    block = pl.BlockSpec((1,) + own.shape[1:], lambda v, s: (v, 0, 0, 0, 0))
    whole = lambda array: pl.BlockSpec(array.shape, lambda v, s: (0,) * array.ndim)
    return pl.pallas_call(
        temporal_kernel,
        grid_spec=pltpu.PrefetchScalarGridSpec(
            num_scalar_prefetch=1,
            grid=(own.shape[0],),
            in_specs=[block, block, whole(temporal_qk), whole(temporal_v), whole(temporal_out)],
            out_specs=block,
        ),
        out_shape=jax.ShapeDtypeStruct(own.shape, jnp.bfloat16),
        compiler_params=pltpu.CompilerParams(vmem_limit_bytes=VMEM_LIMIT),
        cost_estimate=pl.CostEstimate(
            flops=own.shape[0] * 700_000_000, bytes_accessed=2_000_000, transcendentals=0
        ),
        name="temporal",
    )(side, own, other, temporal_qk, temporal_v, temporal_out)


def gelu(values):
    inner = values * (0.7978845608028654 + 0.035677408136300125 * (values * values))
    half = 0.5 * values
    return half + half * jnp.tanh(inner)


def mlp_kernel(left, side_ref, rows_ref, top_ref, bottom_ref, up_ref, mix_ref, down_ref, out_ref):
    _, _, frames, window, channels = rows_ref.shape
    hidden_size = up_ref.shape[1]
    chunk = 256
    side = side_ref[0]
    for frame in range(frames):
        middle = rows_ref[0, :, frame].reshape(2 * window, channels)
        rows = jnp.concatenate([top_ref[0, frame], middle, bottom_ref[0, frame]], axis=0)
        normed = layer_norm(rows.astype(jnp.float32))
        update = jnp.zeros((2 * window, channels), jnp.float32)
        for start in range(0, hidden_size, chunk):
            lanes = slice(start, start + chunk)
            hidden = gelu(dot_dims(normed, up_ref[:, lanes], 1, 0))
            hidden = hidden.astype(jnp.bfloat16).astype(jnp.float32)
            lines = [hidden[line * window : (line + 1) * window] for line in range(4)]
            taps = mix_ref[:, :, lanes].astype(jnp.float32)
            mixed = []
            for line in range(2):
                columns = [
                    functools.reduce(
                        jnp.add, [lines[line + a] * taps[a, b][None] for a in range(3)]
                    )
                    for b in range(3)
                ]
                mixed.append(
                    (
                        pltpu.roll(columns[0], 1, 0)
                        + columns[1]
                        + pltpu.roll(columns[2], window - 1, 0)
                    ).astype(jnp.bfloat16)
                )
            update = update + dot_dims(jnp.concatenate(mixed, axis=0), down_ref[lanes], 1, 0)
        result = middle.astype(jnp.float32) + update
        for line in range(2):
            shifted = pltpu.roll(result[line * window : (line + 1) * window], window - left, 0)
            out_ref[0, side ^ line, frame] = shifted.astype(jnp.bfloat16)


def mlp(side, left, rows, top, bottom, mlp_up, mix_kernel, mlp_down):
    block = pl.BlockSpec((1,) + rows.shape[1:], lambda v, s: (v, 0, 0, 0, 0))
    line = pl.BlockSpec((1,) + top.shape[1:], lambda v, s: (v, 0, 0, 0))
    whole = lambda array: pl.BlockSpec(array.shape, lambda v, s: (0,) * array.ndim)
    return pl.pallas_call(
        functools.partial(mlp_kernel, left),
        grid_spec=pltpu.PrefetchScalarGridSpec(
            num_scalar_prefetch=1,
            grid=(rows.shape[0],),
            in_specs=[block, line, line, whole(mlp_up), whole(mix_kernel), whole(mlp_down)],
            out_specs=block,
        ),
        out_shape=jax.ShapeDtypeStruct(rows.shape, jnp.bfloat16),
        compiler_params=pltpu.CompilerParams(vmem_limit_bytes=VMEM_LIMIT),
        cost_estimate=pl.CostEstimate(
            flops=rows.shape[0] * 1_000_000_000, bytes_accessed=3_000_000, transcendentals=0
        ),
        name="mlp",
    )(side, rows, top, bottom, mlp_up, mix_kernel, mlp_down)


VIEW_GROUPS = ((0, 2),)


def shards(
    video,
    stereo_qk,
    stereo_v,
    stereo_out,
    temporal_qk,
    temporal_v,
    temporal_out,
    mlp_up,
    mix_kernel,
    mlp_down,
):
    width, channels = video.shape[-2:]
    frame_size, rows_size = lax.axis_size("frame"), lax.axis_size("rows")
    pairs = frame_size // 2
    owners = frame_size
    cols = width // owners
    window = round_up(cols + 2, 16)
    left = (window - cols) // 2
    frame, row = lax.axis_index("frame"), lax.axis_index("rows")
    pair, side = frame // 2, row % 2
    side_arg = side.astype(jnp.int32)[None]
    both = ("frame", "rows")
    slots = [(s, p) for s in range(2) for p in range(pairs)]

    def owner_at(s, p):
        return lax.rem(pair + p, pairs) * 2 + (side ^ s)

    def chip_moves(s, p):
        return [
            (
                f * rows_size + r,
                ((f // 2 + p) % pairs * 2 + f % 2) * rows_size + (r ^ s),
            )
            for f in range(frame_size)
            for r in range(rows_size)
        ]

    siblings = [(f, f ^ 1) for f in range(frame_size)]
    upward = [(r, r + 2) for r in range(rows_size - 2)]
    downward = [(r + 2, r) for r in range(rows_size - 2)]
    outputs = []
    for first, count in VIEW_GROUPS:
        windows = stereo(
            video, first, count, owners, left, window, stereo_qk, stereo_v, stereo_out
        )
        pieces = []
        for s, p in slots:
            piece = lax.dynamic_index_in_dim(windows, owner_at(s, p), 1, keepdims=False)
            if (s, p) != (0, 0):
                piece = lax.ppermute(piece, both, chip_moves(s, p))
            pieces.append(piece)
        own = jnp.stack(pieces, axis=1).reshape(count, 2, pairs, window, channels)
        other = lax.ppermute(own, "frame", siblings)
        section = temporal(side_arg, own, other, temporal_qk, temporal_v, temporal_out)
        top = lax.ppermute(section[:, 1], "rows", upward)
        bottom = lax.ppermute(section[:, 0], "rows", downward)
        result = mlp(side_arg, left, section, top, bottom, mlp_up, mix_kernel, mlp_down)
        output = jnp.zeros((count, width, channels), jnp.bfloat16)
        for s, p in slots:
            piece = result[:, s, p, :cols]
            if (s, p) != (0, 0):
                back = [(j, i) for i, j in chip_moves(s, p)]
                piece = lax.ppermute(piece, both, back)
            output = lax.dynamic_update_slice(output, piece, (0, owner_at(s, p) * cols, 0))
        outputs.append(output)
    return jnp.concatenate(outputs, axis=0).reshape(video.shape)


def solution(mesh):
    in_specs = (P(None, "frame", "rows", None, None), P(), P(), P(), P(), P(), P(), P(), P(), P())
    out_specs = P(None, "frame", "rows", None, None)
    return jax.shard_map(shards, mesh=mesh, in_specs=in_specs, out_specs=out_specs, check_vma=False)
```

```python
import functools

import jax
import jax.numpy as jnp
from jax import lax
from jax.experimental import pallas as pl
from jax.experimental.pallas import tpu as pltpu
from jax.sharding import PartitionSpec as P

HEADS = 8
HEAD_DIM = 32
SCALE_LOG2 = HEAD_DIM ** (-0.5) * 1.4426950408889634
VMEM_LIMIT = 40 * 1024 * 1024


def round_up(value, unit):
    return (value + unit - 1) // unit * unit


def layer_norm(widened):
    centred = widened - jnp.mean(widened, axis=-1, keepdims=True)
    variance = jnp.mean(centred * centred, axis=-1, keepdims=True)
    return (centred * lax.rsqrt(variance + 1e-05)).astype(jnp.bfloat16)


def dot_dims(lhs, rhs, lhs_dim, rhs_dim):
    return lax.dot_general(
        lhs, rhs, (((lhs_dim,), (rhs_dim,)), ((), ())), preferred_element_type=jnp.float32
    )


def stereo_kernel(
    left, cols, window, video_hbm, qk_hbm, v_hbm, out_hbm, windows_ref, video_ref, qk_ref, v_ref, out_ref, sems
):
    copies = [
        pltpu.make_async_copy(source, target, sems.at[index])
        for index, (source, target) in enumerate(
            [(video_hbm, video_ref), (qk_hbm, qk_ref), (v_hbm, v_ref), (out_hbm, out_ref)]
        )
    ]
    for copy in copies:
        copy.start()
    for copy in copies:
        copy.wait()
    views = video_ref.shape[0]
    width, channels = video_ref.shape[-2:]
    rows = [video_ref[v].reshape(width, channels).astype(jnp.float32) for v in range(views)]
    normed = [layer_norm(view_rows) for view_rows in rows]
    queries = [dot_dims(n, qk_ref[:, :channels], 1, 0).astype(jnp.bfloat16) for n in normed]
    keys = [dot_dims(n, qk_ref[:, channels:], 1, 0).astype(jnp.bfloat16) for n in normed]
    values = [dot_dims(n, v_ref[...], 1, 0).astype(jnp.bfloat16) for n in normed]
    lane_head = lax.broadcasted_iota(jnp.int32, (width, 128), 1) // HEAD_DIM
    zero = jnp.zeros((), jnp.bfloat16)
    ones = jnp.ones((width, 128), jnp.bfloat16)
    owners = width // cols
    tail = round_up((owners - 1) * cols + window, 8) - width
    for view in range(views):
        groups = []
        for start in range(0, channels, 128):
            lanes = slice(start, start + 128)
            total = jnp.zeros((width, 128), jnp.float32)
            for head in range(128 // HEAD_DIM):
                mask = lane_head == head
                scores = dot_dims(
                    queries[view][:, lanes], jnp.where(mask, keys[1 - view][:, lanes], zero), 1, 1
                )
                top = jnp.max(scores, axis=1, keepdims=True)
                weights = jnp.exp2((scores - top) * SCALE_LOG2).astype(jnp.bfloat16)
                values_head = jnp.where(mask, values[1 - view][:, lanes], zero)
                mixed = dot_dims(weights, jnp.concatenate([values_head, ones], axis=1), 1, 0)
                total = total + mixed[:, :128] * (1.0 / mixed[:, 128:])
            groups.append(total.astype(jnp.bfloat16))
        update = dot_dims(jnp.concatenate(groups, axis=1), out_ref[...], 1, 0)
        section = rows[view] + update
        padded = jnp.concatenate([section, jnp.zeros((tail, channels), jnp.float32)], axis=0)
        padded = pltpu.roll(padded, left, 0)
        for owner in range(owners):
            windows_ref[view, owner] = padded[owner * cols : owner * cols + window].astype(
                jnp.bfloat16
            )


def stereo(video, owners, left, window, *weights):
    views = video.shape[0]
    width, channels = video.shape[-2:]
    operands = [pltpu.with_memory_space_constraint(array, pltpu.HBM) for array in (video, *weights)]
    return pl.pallas_call(
        functools.partial(stereo_kernel, left, width // owners, window),
        in_specs=[pl.BlockSpec(memory_space=pltpu.HBM)] * len(operands),
        out_specs=pl.BlockSpec(memory_space=pltpu.VMEM),
        out_shape=jax.ShapeDtypeStruct((views, owners, window, channels), jnp.bfloat16),
        scratch_shapes=[pltpu.VMEM(array.shape, array.dtype) for array in operands]
        + [pltpu.SemaphoreType.DMA((len(operands),))],
        compiler_params=pltpu.CompilerParams(vmem_limit_bytes=VMEM_LIMIT),
        cost_estimate=pl.CostEstimate(
            flops=2_400_000_000, bytes_accessed=2_000_000, transcendentals=4_000_000
        ),
        name="stereo",
    )(*operands)


def head_sum(product):
    channels, width = product.shape
    return jnp.sum(product.reshape(HEADS, HEAD_DIM, width), axis=1, keepdims=True)


def temporal_kernel(side_ref, own_ref, other_ref, qk_ref, v_ref, out_ref, section_ref):
    _, _, frames, window, channels = own_ref.shape
    side = side_ref[0]
    for slot in range(2):
        rows = own_ref[0, slot].reshape(frames * window, channels).astype(jnp.float32)
        rows_other = other_ref[0, slot].reshape(frames * window, channels).astype(jnp.float32)
        normed = layer_norm(rows)
        normed_all = jnp.concatenate([normed, layer_norm(rows_other)], axis=0)
        queries = dot_dims(qk_ref[:, :channels], normed, 0, 1).astype(jnp.bfloat16)
        keys = dot_dims(qk_ref[:, channels:], normed_all, 0, 1).astype(jnp.bfloat16)
        values = dot_dims(v_ref[...], normed_all, 0, 1).astype(jnp.bfloat16)
        attended = []
        for frame in range(frames):
            query = queries[:, frame * window : (frame + 1) * window].astype(jnp.float32)
            scores = [
                head_sum(
                    query * keys[:, other * window : (other + 1) * window].astype(jnp.float32)
                )
                for other in range(2 * frames)
            ]
            top = functools.reduce(jnp.maximum, scores)
            weights = [jnp.exp2((score - top) * SCALE_LOG2) for score in scores]
            inverse = 1.0 / functools.reduce(jnp.add, weights)
            mixed = jnp.zeros((HEADS, HEAD_DIM, window), jnp.float32)
            for other in range(2 * frames):
                value = values[:, other * window : (other + 1) * window].astype(jnp.float32)
                mixed = mixed + value.reshape(HEADS, HEAD_DIM, window) * (
                    weights[other] * inverse
                )
            attended.append(mixed.reshape(channels, window).astype(jnp.bfloat16))
        update = dot_dims(jnp.concatenate(attended, axis=1), out_ref[...], 0, 0)
        section = (rows + update).astype(jnp.bfloat16)
        section_ref[0, side ^ slot] = section.reshape(frames, window, channels)


def temporal(side, own, other, temporal_qk, temporal_v, temporal_out):
    block = pl.BlockSpec((1,) + own.shape[1:], lambda v, s: (v, 0, 0, 0, 0))
    whole = lambda array: pl.BlockSpec(array.shape, lambda v, s: (0,) * array.ndim)
    return pl.pallas_call(
        temporal_kernel,
        grid_spec=pltpu.PrefetchScalarGridSpec(
            num_scalar_prefetch=1,
            grid=(own.shape[0],),
            in_specs=[block, block, whole(temporal_qk), whole(temporal_v), whole(temporal_out)],
            out_specs=block,
        ),
        out_shape=jax.ShapeDtypeStruct(own.shape, jnp.bfloat16),
        compiler_params=pltpu.CompilerParams(vmem_limit_bytes=VMEM_LIMIT),
        cost_estimate=pl.CostEstimate(
            flops=own.shape[0] * 700_000_000, bytes_accessed=2_000_000, transcendentals=0
        ),
        name="temporal",
    )(side, own, other, temporal_qk, temporal_v, temporal_out)


def gelu(values):
    inner = values * (0.7978845608028654 + 0.035677408136300125 * (values * values))
    half = 0.5 * values
    return half + half * jnp.tanh(inner)


def mlp_mix(columns, window):
    return (
        pltpu.roll(columns[0], 1, 0) + columns[1] + pltpu.roll(columns[2], window - 1, 0)
    ).astype(jnp.bfloat16)


def inner_kernel(rows_ref, up_ref, mix_ref, down_ref, partial_ref):
    _, _, frames, window, channels = rows_ref.shape
    chunk = 256
    for frame in range(frames):
        rows = rows_ref[0, :, frame].reshape(2 * window, channels).astype(jnp.float32)
        normed = layer_norm(rows)
        total = rows
        for start in range(0, up_ref.shape[1], chunk):
            lanes = slice(start, start + chunk)
            hidden = gelu(dot_dims(normed, up_ref[:, lanes], 1, 0))
            hidden = hidden.astype(jnp.bfloat16).astype(jnp.float32)
            lines = [hidden[:window], hidden[window:]]
            taps = mix_ref[:, :, lanes].astype(jnp.float32)
            mixed = [
                mlp_mix(
                    [
                        lines[0] * taps[1 - line, b][None] + lines[1] * taps[2 - line, b][None]
                        for b in range(3)
                    ],
                    window,
                )
                for line in range(2)
            ]
            total = total + dot_dims(jnp.concatenate(mixed, axis=0), down_ref[lanes], 1, 0)
        partial_ref[0, :, frame] = total.reshape(2, window, channels)


def outer_kernel(
    left, side_ref, partial_ref, top_ref, bottom_ref, up_ref, mix_ref, down_ref, out_ref
):
    _, _, frames, window, channels = partial_ref.shape
    chunk = 256
    side = side_ref[0]
    for frame in range(frames):
        rows = jnp.concatenate([top_ref[0, frame], bottom_ref[0, frame]], axis=0)
        normed = layer_norm(rows.astype(jnp.float32))
        total = partial_ref[0, :, frame].reshape(2 * window, channels)
        for start in range(0, up_ref.shape[1], chunk):
            lanes = slice(start, start + chunk)
            hidden = gelu(dot_dims(normed, up_ref[:, lanes], 1, 0))
            hidden = hidden.astype(jnp.bfloat16).astype(jnp.float32)
            taps = mix_ref[:, :, lanes].astype(jnp.float32)
            mixed = [
                mlp_mix(
                    [
                        hidden[line * window : (line + 1) * window] * taps[2 * line, b][None]
                        for b in range(3)
                    ],
                    window,
                )
                for line in range(2)
            ]
            total = total + dot_dims(jnp.concatenate(mixed, axis=0), down_ref[lanes], 1, 0)
        for line in range(2):
            shifted = pltpu.roll(total[line * window : (line + 1) * window], window - left, 0)
            out_ref[0, side ^ line, frame] = shifted.astype(jnp.bfloat16)


def inner(rows, mlp_up, mix_kernel, mlp_down):
    block = pl.BlockSpec((1,) + rows.shape[1:], lambda v: (v, 0, 0, 0, 0))
    whole = lambda array: pl.BlockSpec(array.shape, lambda v: (0,) * array.ndim)
    return pl.pallas_call(
        inner_kernel,
        grid=(rows.shape[0],),
        in_specs=[block, whole(mlp_up), whole(mix_kernel), whole(mlp_down)],
        out_specs=block,
        out_shape=jax.ShapeDtypeStruct(rows.shape, jnp.float32),
        compiler_params=pltpu.CompilerParams(vmem_limit_bytes=VMEM_LIMIT),
        cost_estimate=pl.CostEstimate(
            flops=rows.shape[0] * 2_000_000_000, bytes_accessed=3_000_000, transcendentals=0
        ),
        name="inner",
    )(rows, mlp_up, mix_kernel, mlp_down)


def outer(side, left, partial, top, bottom, mlp_up, mix_kernel, mlp_down):
    block = pl.BlockSpec((1,) + partial.shape[1:], lambda v, s: (v, 0, 0, 0, 0))
    line = pl.BlockSpec((1,) + top.shape[1:], lambda v, s: (v, 0, 0, 0))
    whole = lambda array: pl.BlockSpec(array.shape, lambda v, s: (0,) * array.ndim)
    return pl.pallas_call(
        functools.partial(outer_kernel, left),
        grid_spec=pltpu.PrefetchScalarGridSpec(
            num_scalar_prefetch=1,
            grid=(partial.shape[0],),
            in_specs=[block, line, line, whole(mlp_up), whole(mix_kernel), whole(mlp_down)],
            out_specs=block,
        ),
        out_shape=jax.ShapeDtypeStruct(partial.shape, jnp.bfloat16),
        compiler_params=pltpu.CompilerParams(vmem_limit_bytes=VMEM_LIMIT),
        cost_estimate=pl.CostEstimate(
            flops=partial.shape[0] * 1_000_000_000, bytes_accessed=3_000_000, transcendentals=0
        ),
        name="outer",
    )(side, partial, top, bottom, mlp_up, mix_kernel, mlp_down)


def shards(
    video,
    stereo_qk,
    stereo_v,
    stereo_out,
    temporal_qk,
    temporal_v,
    temporal_out,
    mlp_up,
    mix_kernel,
    mlp_down,
):
    width, channels = video.shape[-2:]
    frame_size, rows_size = lax.axis_size("frame"), lax.axis_size("rows")
    pairs = frame_size // 2
    owners = frame_size
    cols = width // owners
    window = round_up(cols + 2, 16)
    left = (window - cols) // 2
    frame, row = lax.axis_index("frame"), lax.axis_index("rows")
    pair, side = frame // 2, row % 2
    side_arg = side.astype(jnp.int32)[None]
    both = ("frame", "rows")
    slots = [(s, p) for s in range(2) for p in range(pairs)]

    def owner_at(s, p):
        return lax.rem(pair + p, pairs) * 2 + (side ^ s)

    def chip_moves(s, p):
        return [
            (
                f * rows_size + r,
                ((f // 2 + p) % pairs * 2 + f % 2) * rows_size + (r ^ s),
            )
            for f in range(frame_size)
            for r in range(rows_size)
        ]

    siblings = [(f, f ^ 1) for f in range(frame_size)]
    upward = [(r, r + 2) for r in range(rows_size - 2)]
    downward = [(r + 2, r) for r in range(rows_size - 2)]
    windows = stereo(video, owners, left, window, stereo_qk, stereo_v, stereo_out)
    pieces = []
    for s, p in slots:
        piece = lax.dynamic_index_in_dim(windows, owner_at(s, p), 1, keepdims=False)
        if (s, p) != (0, 0):
            piece = lax.ppermute(piece, both, chip_moves(s, p))
        pieces.append(piece)
    own = jnp.stack(pieces, axis=1).reshape(-1, 2, pairs, window, channels)
    other = lax.ppermute(own, "frame", siblings)
    section = temporal(side_arg, own, other, temporal_qk, temporal_v, temporal_out)
    top = lax.ppermute(section[:, 1], "rows", upward)
    bottom = lax.ppermute(section[:, 0], "rows", downward)
    partial = inner(section, mlp_up, mix_kernel, mlp_down)
    result = outer(side_arg, left, partial, top, bottom, mlp_up, mix_kernel, mlp_down)
    output = jnp.zeros((video.shape[0], width, channels), jnp.bfloat16)
    for s, p in slots:
        piece = result[:, s, p, :cols]
        if (s, p) != (0, 0):
            back = [(j, i) for i, j in chip_moves(s, p)]
            piece = lax.ppermute(piece, both, back)
        output = lax.dynamic_update_slice(output, piece, (0, owner_at(s, p) * cols, 0))
    return output.reshape(video.shape)


def solution(mesh):
    in_specs = (P(None, "frame", "rows", None, None), P(), P(), P(), P(), P(), P(), P(), P(), P())
    out_specs = P(None, "frame", "rows", None, None)
    return jax.shard_map(shards, mesh=mesh, in_specs=in_specs, out_specs=out_specs, check_vma=False)
```

```python
import functools

import jax
import jax.numpy as jnp
from jax import lax
from jax.experimental import pallas as pl
from jax.experimental.pallas import tpu as pltpu
from jax.sharding import PartitionSpec as P

HEADS = 8
HEAD_DIM = 32
SCALE_LOG2 = HEAD_DIM ** (-0.5) * 1.4426950408889634
VMEM_LIMIT = 40 * 1024 * 1024


def round_up(value, unit):
    return (value + unit - 1) // unit * unit


def layer_norm(widened):
    centred = widened - jnp.mean(widened, axis=-1, keepdims=True)
    variance = jnp.mean(centred * centred, axis=-1, keepdims=True)
    return (centred * lax.rsqrt(variance + 1e-05)).astype(jnp.bfloat16)


def dot_dims(lhs, rhs, lhs_dim, rhs_dim):
    return lax.dot_general(
        lhs, rhs, (((lhs_dim,), (rhs_dim,)), ((), ())), preferred_element_type=jnp.float32
    )


def stereo_rows(left, cols, rows, rows_other, qk_ref, v_ref, out_ref, windows_ref):
    width, channels = rows.shape
    normed = layer_norm(rows)
    normed_other = layer_norm(rows_other)
    queries = dot_dims(normed, qk_ref[:, :channels], 1, 0).astype(jnp.bfloat16)
    keys = dot_dims(normed_other, qk_ref[:, channels:], 1, 0).astype(jnp.bfloat16)
    values = dot_dims(normed_other, v_ref[...], 1, 0).astype(jnp.bfloat16)
    lane_head = lax.broadcasted_iota(jnp.int32, (width, 128), 1) // HEAD_DIM
    zero = jnp.zeros((), jnp.bfloat16)
    ones = jnp.ones((width, 128), jnp.bfloat16)
    owners, window, _ = windows_ref.shape
    tail = round_up((owners - 1) * cols + window, 8) - width
    groups = []
    for start in range(0, channels, 128):
        lanes = slice(start, start + 128)
        total = jnp.zeros((width, 128), jnp.float32)
        for head in range(128 // HEAD_DIM):
            mask = lane_head == head
            scores = dot_dims(queries[:, lanes], jnp.where(mask, keys[:, lanes], zero), 1, 1)
            top = jnp.max(scores, axis=1, keepdims=True)
            weights = jnp.exp2((scores - top) * SCALE_LOG2).astype(jnp.bfloat16)
            values_head = jnp.where(mask, values[:, lanes], zero)
            mixed = dot_dims(weights, jnp.concatenate([values_head, ones], axis=1), 1, 0)
            total = total + mixed[:, :128] * (1.0 / mixed[:, 128:])
        groups.append(total.astype(jnp.bfloat16))
    update = dot_dims(jnp.concatenate(groups, axis=1), out_ref[...], 1, 0)
    padded = jnp.concatenate([rows + update, jnp.zeros((tail, channels), jnp.float32)], axis=0)
    padded = pltpu.roll(padded, left, 0)
    for owner in range(owners):
        windows_ref[owner] = padded[owner * cols : owner * cols + window].astype(jnp.bfloat16)


def first_kernel(left, cols, core_ref, *refs):
    count = (len(refs) - 2) // 2
    sources, windows_ref = refs[:count], refs[count]
    targets, sems = (refs[-2], *refs[count + 1 : -2]), refs[-1]
    copies = [
        pltpu.make_async_copy(source, target, sems.at[index])
        for index, (source, target) in enumerate(zip(sources, targets))
    ]
    for copy in copies:
        copy.start()
    for copy in copies[:4]:
        copy.wait()
    second_kernel(left, cols, core_ref, *targets[:4], windows_ref)
    for copy in copies[4:]:
        copy.wait()


def second_kernel(left, cols, core_ref, video_ref, qk_ref, v_ref, out_ref, windows_ref):
    core = core_ref[0]
    width, channels = video_ref.shape[-2:]
    rows = video_ref[core].reshape(width, channels).astype(jnp.float32)
    rows_other = video_ref[1 - core].reshape(width, channels).astype(jnp.float32)
    stereo_rows(left, cols, rows, rows_other, qk_ref, v_ref, out_ref, windows_ref)


def first_stereo(core, video, owners, left, window, *weights):
    width, channels = video.shape[-2:]
    operands = [pltpu.with_memory_space_constraint(array, pltpu.HBM) for array in (video, *weights)]
    vmem = pl.BlockSpec(memory_space=pltpu.VMEM)
    return pl.pallas_call(
        functools.partial(first_kernel, left, width // owners),
        in_specs=[pl.BlockSpec(memory_space=pltpu.SMEM)]
        + [pl.BlockSpec(memory_space=pltpu.HBM)] * len(operands),
        out_specs=[vmem] * len(operands),
        out_shape=[jax.ShapeDtypeStruct((owners, window, channels), jnp.bfloat16)]
        + [jax.ShapeDtypeStruct(array.shape, array.dtype) for array in weights],
        scratch_shapes=[
            pltpu.VMEM(video.shape, video.dtype),
            pltpu.SemaphoreType.DMA((len(operands),)),
        ],
        compiler_params=pltpu.CompilerParams(vmem_limit_bytes=VMEM_LIMIT),
        cost_estimate=pl.CostEstimate(
            flops=2_400_000_000, bytes_accessed=2_000_000, transcendentals=2_000_000
        ),
        name="stereo",
    )(core, *operands)


def head_sum(product):
    channels, width = product.shape
    return jnp.sum(product.reshape(HEADS, HEAD_DIM, width), axis=1, keepdims=True)


def temporal_kernel(pairs, *refs):
    pieces, (qk_ref, v_ref, out_ref, section_ref) = refs[:pairs], refs[pairs:]
    _, pair_size, window, channels = section_ref.shape
    frames = pairs * pair_size
    rows = jnp.concatenate(
        [piece[...].reshape(pair_size * window, channels) for piece in pieces], axis=0
    ).astype(jnp.float32)
    normed = layer_norm(rows)
    queries = dot_dims(qk_ref[:, :channels], normed, 0, 1).astype(jnp.bfloat16)
    keys = dot_dims(qk_ref[:, channels:], normed, 0, 1).astype(jnp.bfloat16)
    values = dot_dims(v_ref[...], normed, 0, 1).astype(jnp.bfloat16)
    attended = []
    for frame in range(frames):
        query = queries[:, frame * window : (frame + 1) * window].astype(jnp.float32)
        scores = [
            head_sum(query * keys[:, other * window : (other + 1) * window].astype(jnp.float32))
            for other in range(frames)
        ]
        top = functools.reduce(jnp.maximum, scores)
        weights = [jnp.exp2((score - top) * SCALE_LOG2) for score in scores]
        inverse = 1.0 / functools.reduce(jnp.add, weights)
        mixed = jnp.zeros((HEADS, HEAD_DIM, window), jnp.float32)
        for other in range(frames):
            value = values[:, other * window : (other + 1) * window].astype(jnp.float32)
            mixed = mixed + value.reshape(HEADS, HEAD_DIM, window) * (weights[other] * inverse)
        attended.append(mixed.reshape(channels, window).astype(jnp.bfloat16))
    update = dot_dims(jnp.concatenate(attended, axis=1), out_ref[...], 0, 0)
    section_ref[...] = (rows + update).astype(jnp.bfloat16).reshape(section_ref.shape)


def kernel_call(body, name, flops, out_shape, scalars, *operands):
    return pl.pallas_call(
        body,
        in_specs=[pl.BlockSpec(memory_space=pltpu.SMEM)] * len(scalars)
        + [pl.BlockSpec(memory_space=pltpu.VMEM)] * len(operands),
        out_specs=jax.tree.map(lambda _: pl.BlockSpec(memory_space=pltpu.VMEM), out_shape),
        out_shape=out_shape,
        compiler_params=pltpu.CompilerParams(vmem_limit_bytes=VMEM_LIMIT),
        cost_estimate=pl.CostEstimate(flops=flops, bytes_accessed=3_000_000, transcendentals=0),
        name=name,
    )(*scalars, *operands)


def gelu(values):
    inner = values * (0.7978845608028654 + 0.035677408136300125 * (values * values))
    half = 0.5 * values
    return half + half * jnp.tanh(inner)


def mlp_mix(columns, window):
    return (
        pltpu.roll(columns[0], 1, 0) + columns[1] + pltpu.roll(columns[2], window - 1, 0)
    ).astype(jnp.bfloat16)


CHUNK = 256


def mlp_hidden(normed, up_ref, start):
    hidden = gelu(dot_dims(normed, up_ref[:, start : start + CHUNK], 1, 0))
    return hidden.astype(jnp.bfloat16).astype(jnp.float32)


def inner_kernel(side_ref, own_ref, next_ref, up_ref, mix_ref, down_ref, *partial_refs):
    pairs, pair_size, window, channels = own_ref.shape
    other_tap = (2 - 2 * side_ref[0], 2 * side_ref[0])
    for pair in range(pairs):
        for member in range(pair_size):
            rows = jnp.concatenate([own_ref[pair, member], next_ref[pair, member]], axis=0)
            rows = rows.astype(jnp.float32)
            normed = layer_norm(rows)
            total = rows
            for start in range(0, up_ref.shape[1], CHUNK):
                lanes = slice(start, start + CHUNK)
                hidden = mlp_hidden(normed, up_ref, start)
                lines = [hidden[:window], hidden[window:]]
                same = mix_ref[1, :, lanes].astype(jnp.float32)
                mixed = []
                for slot in range(2):
                    across = mix_ref[other_tap[slot], :, lanes].astype(jnp.float32)
                    mixed.append(
                        mlp_mix(
                            [
                                lines[slot] * same[b][None] + lines[1 - slot] * across[b][None]
                                for b in range(3)
                            ],
                            window,
                        )
                    )
                total = total + dot_dims(jnp.concatenate(mixed, axis=0), down_ref[lanes], 1, 0)
            for slot in range(2):
                partial_refs[slot][pair, member] = total[slot * window : (slot + 1) * window]


def outer_kernel(
    left, slot, side_ref, edge_ref, partial_ref, halo_ref, up_ref, mix_ref, down_ref, own_ref, sibling_ref
):
    pairs, pair_size, window, channels = partial_ref.shape
    tap = 2 * side_ref[0] if slot == 0 else 2 - 2 * side_ref[0]
    for pair in range(pairs):
        rows = halo_ref[pair].reshape(pair_size * window, channels).astype(jnp.float32)
        normed = layer_norm(jnp.where(edge_ref[0] == 1, jnp.zeros_like(rows), rows))
        total = partial_ref[pair].reshape(pair_size * window, channels)
        for start in range(0, up_ref.shape[1], CHUNK):
            lanes = slice(start, start + CHUNK)
            hidden = mlp_hidden(normed, up_ref, start)
            across = mix_ref[tap, :, lanes].astype(jnp.float32)
            mixed = [
                mlp_mix(
                    [
                        hidden[member * window : (member + 1) * window] * across[b][None]
                        for b in range(3)
                    ],
                    window,
                )
                for member in range(pair_size)
            ]
            total = total + dot_dims(jnp.concatenate(mixed, axis=0), down_ref[lanes], 1, 0)
        for member, ref in enumerate((own_ref, sibling_ref)):
            shifted = pltpu.roll(total[member * window : (member + 1) * window], window - left, 0)
            ref[pair] = shifted.astype(jnp.bfloat16)


def shards(
    video,
    stereo_qk,
    stereo_v,
    stereo_out,
    temporal_qk,
    temporal_v,
    temporal_out,
    mlp_up,
    mix_kernel,
    mlp_down,
):
    width, channels = video.shape[-2:]
    frame_size, rows_size = lax.axis_size("frame"), lax.axis_size("rows")
    pairs = frame_size // 2
    owners = frame_size
    cols = width // owners
    window = round_up(cols + 2, 16)
    left = (window - cols) // 2
    frame, row = lax.axis_index("frame"), lax.axis_index("rows")
    pair, side = frame // 2, row % 2
    side_arg = side.astype(jnp.int32)[None]
    both = ("frame", "rows")
    slots = [(s, p) for s in range(2) for p in range(pairs)]

    def owner_at(s, p):
        return lax.rem(pair + p, pairs) * 2 + (side ^ s)

    def chip_moves(s, p):
        return [
            (
                f * rows_size + r,
                ((f // 2 + p) % pairs * 2 + f % 2) * rows_size + (r ^ s),
            )
            for f in range(frame_size)
            for r in range(rows_size)
        ]

    siblings = [(f, f ^ 1) for f in range(frame_size)]
    bands = rows_size // 2
    band_moves = []
    for slot in range(2):
        moves = []
        for r in range(rows_size):
            band = r // 2 + (1 if (r + slot) % 2 else -1)
            moves.append((r, band * 2 + r % 2 if 0 <= band < bands else r ^ 1))
        band_moves.append(moves)
    first_band, last_band = row // 2 == 0, row // 2 == bands - 1
    at_edge = (
        jnp.where(side == 0, last_band, first_band),
        jnp.where(side == 0, first_band, last_band),
    )
    edge_args = [edge.astype(jnp.int32)[None] for edge in at_edge]
    core_arg = (frame % 2).astype(jnp.int32)[None]
    sibling_video = lax.ppermute(video, "frame", siblings)
    windows, *weights = first_stereo(
        core_arg,
        video,
        owners,
        left,
        window,
        stereo_qk,
        stereo_v,
        stereo_out,
        temporal_qk,
        temporal_v,
        temporal_out,
    )
    sibling_windows = kernel_call(
        functools.partial(second_kernel, left, cols),
        "stereo",
        2_400_000_000,
        jax.ShapeDtypeStruct(windows.shape, windows.dtype),
        (core_arg,),
        sibling_video,
        *weights[:3],
    )
    pieces = {}
    for s, p in slots:
        index = owner_at(s, p)
        piece = jnp.stack(
            [
                lax.dynamic_index_in_dim(array, index, 0, keepdims=False)
                for array in (windows, sibling_windows)
            ]
        )
        if (s, p) != (0, 0):
            piece = lax.ppermute(piece, both, chip_moves(s, p))
        pieces[s, p] = piece
    shape = (pairs, 2, window, channels)
    sections, halos = [], []
    for s in range(2):
        section = kernel_call(
            functools.partial(temporal_kernel, pairs),
            "temporal",
            1_000_000_000,
            jax.ShapeDtypeStruct(shape, jnp.bfloat16),
            (),
            *[pieces[s, p] for p in range(pairs)],
            *weights[3:],
        )
        sections.append(section)
        halos.append(lax.ppermute(section, "rows", band_moves[s]))
    partials = kernel_call(
        inner_kernel,
        "inner",
        4_000_000_000,
        [jax.ShapeDtypeStruct(shape, jnp.float32)] * 2,
        (side_arg,),
        *sections,
        mlp_up,
        mix_kernel,
        mlp_down,
    )
    output = jnp.zeros((video.shape[0], width, channels), jnp.bfloat16)
    for s in (1, 0):
        own_out, sibling_out = kernel_call(
            functools.partial(outer_kernel, left, s),
            "outer",
            1_000_000_000,
            [jax.ShapeDtypeStruct((pairs, window, channels), jnp.bfloat16)] * 2,
            (side_arg, edge_args[1 - s]),
            partials[s],
            halos[1 - s],
            mlp_up,
            mix_kernel,
            mlp_down,
        )
        other_out = lax.ppermute(sibling_out, "frame", siblings)
        first_view = jnp.where(frame % 2 == 0, own_out, other_out)
        second_view = jnp.where(frame % 2 == 0, other_out, own_out)
        for p in range(pairs):
            piece = jnp.stack([first_view[p, :cols], second_view[p, :cols]])
            if (s, p) != (0, 0):
                back = [(j, i) for i, j in chip_moves(s, p)]
                piece = lax.ppermute(piece, both, back)
            output = lax.dynamic_update_slice(output, piece, (0, owner_at(s, p) * cols, 0))
    return output.reshape(video.shape)


def solution(mesh):
    in_specs = (P(None, "frame", "rows", None, None), P(), P(), P(), P(), P(), P(), P(), P(), P())
    out_specs = P(None, "frame", "rows", None, None)
    return jax.shard_map(shards, mesh=mesh, in_specs=in_specs, out_specs=out_specs, check_vma=False)
```

```python
import functools

import jax
import jax.numpy as jnp
from jax import lax
from jax.experimental import pallas as pl
from jax.experimental.pallas import tpu as pltpu
from jax.sharding import PartitionSpec as P

HEADS = 8
HEAD_DIM = 32
SCALE_LOG2 = HEAD_DIM ** (-0.5) * 1.4426950408889634
VMEM_LIMIT = 40 * 1024 * 1024


def round_up(value, unit):
    return (value + unit - 1) // unit * unit


def layer_norm(widened):
    centred = widened - jnp.mean(widened, axis=-1, keepdims=True)
    variance = jnp.mean(centred * centred, axis=-1, keepdims=True)
    return (centred * lax.rsqrt(variance + 1e-05)).astype(jnp.bfloat16)


def dot_dims(lhs, rhs, lhs_dim, rhs_dim):
    return lax.dot_general(
        lhs, rhs, (((lhs_dim,), (rhs_dim,)), ((), ())), preferred_element_type=jnp.float32
    )


def stereo_rows(left, cols, rows, rows_other, qk_ref, v_ref, out_ref, windows_ref):
    width, channels = rows.shape
    normed = layer_norm(rows)
    normed_other = layer_norm(rows_other)
    queries = dot_dims(normed, qk_ref[:, :channels], 1, 0).astype(jnp.bfloat16)
    keys = dot_dims(normed_other, qk_ref[:, channels:], 1, 0).astype(jnp.bfloat16)
    values = dot_dims(normed_other, v_ref[...], 1, 0).astype(jnp.bfloat16)
    lane_head = lax.broadcasted_iota(jnp.int32, (width, 128), 1) // HEAD_DIM
    zero = jnp.zeros((), jnp.bfloat16)
    ones = jnp.ones((width, 128), jnp.bfloat16)
    owners, window, _ = windows_ref.shape
    tail = round_up((owners - 1) * cols + window, 8) - width
    groups = []
    for start in range(0, channels, 128):
        lanes = slice(start, start + 128)
        total = jnp.zeros((width, 128), jnp.float32)
        for head in range(128 // HEAD_DIM):
            mask = lane_head == head
            scores = dot_dims(queries[:, lanes], jnp.where(mask, keys[:, lanes], zero), 1, 1)
            top = jnp.max(scores, axis=1, keepdims=True)
            weights = jnp.exp2((scores - top) * SCALE_LOG2).astype(jnp.bfloat16)
            values_head = jnp.where(mask, values[:, lanes], zero)
            mixed = dot_dims(weights, jnp.concatenate([values_head, ones], axis=1), 1, 0)
            total = total + mixed[:, :128] * (1.0 / mixed[:, 128:])
        groups.append(total.astype(jnp.bfloat16))
    update = dot_dims(jnp.concatenate(groups, axis=1), out_ref[...], 1, 0)
    padded = jnp.concatenate([rows + update, jnp.zeros((tail, channels), jnp.float32)], axis=0)
    padded = pltpu.roll(padded, left, 0)
    for owner in range(owners):
        windows_ref[owner] = padded[owner * cols : owner * cols + window].astype(jnp.bfloat16)


def first_kernel(left, cols, core_ref, *refs):
    count = (len(refs) - 2) // 2
    sources, windows_ref = refs[:count], refs[count]
    targets, sems = (refs[-2], *refs[count + 1 : -2]), refs[-1]
    copies = [
        pltpu.make_async_copy(source, target, sems.at[index])
        for index, (source, target) in enumerate(zip(sources, targets))
    ]
    for copy in copies:
        copy.start()
    for copy in copies[:4]:
        copy.wait()
    second_kernel(left, cols, core_ref, *targets[:4], windows_ref)
    for copy in copies[4:]:
        copy.wait()


def second_kernel(left, cols, core_ref, video_ref, qk_ref, v_ref, out_ref, windows_ref):
    core = core_ref[0]
    width, channels = video_ref.shape[-2:]
    rows = video_ref[core].reshape(width, channels).astype(jnp.float32)
    rows_other = video_ref[1 - core].reshape(width, channels).astype(jnp.float32)
    stereo_rows(left, cols, rows, rows_other, qk_ref, v_ref, out_ref, windows_ref)


def first_stereo(core, video, owners, left, window, *weights):
    width, channels = video.shape[-2:]
    operands = [pltpu.with_memory_space_constraint(array, pltpu.HBM) for array in (video, *weights)]
    vmem = pl.BlockSpec(memory_space=pltpu.VMEM)
    return pl.pallas_call(
        functools.partial(first_kernel, left, width // owners),
        in_specs=[pl.BlockSpec(memory_space=pltpu.SMEM)]
        + [pl.BlockSpec(memory_space=pltpu.HBM)] * len(operands),
        out_specs=[vmem] * len(operands),
        out_shape=[jax.ShapeDtypeStruct((owners, window, channels), jnp.bfloat16)]
        + [jax.ShapeDtypeStruct(array.shape, array.dtype) for array in weights],
        scratch_shapes=[
            pltpu.VMEM(video.shape, video.dtype),
            pltpu.SemaphoreType.DMA((len(operands),)),
        ],
        compiler_params=pltpu.CompilerParams(vmem_limit_bytes=VMEM_LIMIT),
        cost_estimate=pl.CostEstimate(
            flops=2_400_000_000, bytes_accessed=2_000_000, transcendentals=2_000_000
        ),
        name="stereo",
    )(core, *operands)


def head_sum(product):
    channels, width = product.shape
    return jnp.sum(product.reshape(HEADS, HEAD_DIM, width), axis=1, keepdims=True)


def temporal_kernel(pairs, order, *refs):
    pieces, (qk_ref, v_ref, out_ref, section_ref) = refs[:pairs][::order], refs[pairs:]
    _, pair_size, window, channels = section_ref.shape
    frames = pairs * pair_size
    rows = jnp.concatenate(
        [piece[...].reshape(pair_size * window, channels) for piece in pieces], axis=0
    ).astype(jnp.float32)
    normed = layer_norm(rows)
    queries = dot_dims(qk_ref[:, :channels], normed, 0, 1).astype(jnp.bfloat16)
    keys = dot_dims(qk_ref[:, channels:], normed, 0, 1).astype(jnp.bfloat16)
    values = dot_dims(v_ref[...], normed, 0, 1).astype(jnp.bfloat16)
    attended = []
    for frame in range(frames):
        query = queries[:, frame * window : (frame + 1) * window].astype(jnp.float32)
        scores = [
            head_sum(query * keys[:, other * window : (other + 1) * window].astype(jnp.float32))
            for other in range(frames)
        ]
        top = functools.reduce(jnp.maximum, scores)
        weights = [jnp.exp2((score - top) * SCALE_LOG2) for score in scores]
        inverse = 1.0 / functools.reduce(jnp.add, weights)
        mixed = jnp.zeros((HEADS, HEAD_DIM, window), jnp.float32)
        for other in range(frames):
            value = values[:, other * window : (other + 1) * window].astype(jnp.float32)
            mixed = mixed + value.reshape(HEADS, HEAD_DIM, window) * (weights[other] * inverse)
        attended.append(mixed.reshape(channels, window).astype(jnp.bfloat16))
    update = dot_dims(jnp.concatenate(attended, axis=1), out_ref[...], 0, 0)
    section_ref[...] = (rows + update).astype(jnp.bfloat16).reshape(section_ref.shape)


def kernel_call(body, name, flops, out_shape, scalars, *operands, after=()):
    count = len(scalars) + len(operands)

    def ordered_body(*refs):
        body(*refs[:count], *refs[count + len(after) :])

    return pl.pallas_call(
        ordered_body,
        in_specs=[pl.BlockSpec(memory_space=pltpu.SMEM)] * len(scalars)
        + [pl.BlockSpec(memory_space=pltpu.VMEM)] * len(operands)
        + [pl.BlockSpec(memory_space=pl.ANY)] * len(after),
        out_specs=jax.tree.map(lambda _: pl.BlockSpec(memory_space=pltpu.VMEM), out_shape),
        out_shape=out_shape,
        compiler_params=pltpu.CompilerParams(vmem_limit_bytes=VMEM_LIMIT),
        cost_estimate=pl.CostEstimate(flops=flops, bytes_accessed=3_000_000, transcendentals=0),
        name=name,
    )(*scalars, *operands, *after)


def double_gelu(values):
    inner = values * (
        jnp.bfloat16(0.7978845608028654) + jnp.bfloat16(0.035677408136300125) * (values * values)
    )
    return values + values * jnp.tanh(inner)


def half_taps(mix_ref, tap, lanes):
    return mix_ref[tap, :, lanes] * jnp.bfloat16(0.5)


def mlp_mix(columns, window):
    columns = [column.astype(jnp.float32) for column in columns]
    return (
        pltpu.roll(columns[0], 1, 0) + columns[1] + pltpu.roll(columns[2], window - 1, 0)
    ).astype(jnp.bfloat16)


CHUNK = 256


def mlp_hidden(normed, up_ref, start):
    product = dot_dims(normed, up_ref[:, start : start + CHUNK], 1, 0)
    return double_gelu(product.astype(jnp.bfloat16))


def inner_kernel(side_ref, own_ref, next_ref, up_ref, mix_ref, down_ref, *partial_refs):
    pairs, pair_size, window, channels = own_ref.shape
    other_tap = (2 - 2 * side_ref[0], 2 * side_ref[0])
    for pair in range(pairs):
        for member in range(pair_size):
            rows = jnp.concatenate([own_ref[pair, member], next_ref[pair, member]], axis=0)
            rows = rows.astype(jnp.float32)
            normed = layer_norm(rows)
            total = rows
            for start in range(0, up_ref.shape[1], CHUNK):
                lanes = slice(start, start + CHUNK)
                hidden = mlp_hidden(normed, up_ref, start)
                lines = [hidden[:window], hidden[window:]]
                same = half_taps(mix_ref, 1, lanes)
                mixed = []
                for slot in range(2):
                    across = half_taps(mix_ref, other_tap[slot], lanes)
                    mixed.append(
                        mlp_mix(
                            [
                                lines[slot] * same[b][None] + lines[1 - slot] * across[b][None]
                                for b in range(3)
                            ],
                            window,
                        )
                    )
                total = total + dot_dims(jnp.concatenate(mixed, axis=0), down_ref[lanes], 1, 0)
            for slot in range(2):
                partial_refs[slot][pair, member] = total[slot * window : (slot + 1) * window]


def outer_kernel(
    left, slot, side_ref, edge_ref, partial_ref, halo_ref, up_ref, mix_ref, down_ref, own_ref, sibling_ref
):
    pairs, pair_size, window, channels = partial_ref.shape
    tap = 2 * side_ref[0] if slot == 0 else 2 - 2 * side_ref[0]
    for pair in range(pairs):
        rows = halo_ref[pair].reshape(pair_size * window, channels).astype(jnp.float32)
        normed = layer_norm(jnp.where(edge_ref[0] == 1, jnp.zeros_like(rows), rows))
        total = partial_ref[pair].reshape(pair_size * window, channels)
        for start in range(0, up_ref.shape[1], CHUNK):
            lanes = slice(start, start + CHUNK)
            hidden = mlp_hidden(normed, up_ref, start)
            across = half_taps(mix_ref, tap, lanes)
            mixed = [
                mlp_mix(
                    [
                        hidden[member * window : (member + 1) * window] * across[b][None]
                        for b in range(3)
                    ],
                    window,
                )
                for member in range(pair_size)
            ]
            total = total + dot_dims(jnp.concatenate(mixed, axis=0), down_ref[lanes], 1, 0)
        for member, ref in enumerate((own_ref, sibling_ref)):
            shifted = pltpu.roll(total[member * window : (member + 1) * window], window - left, 0)
            ref[pair] = shifted.astype(jnp.bfloat16)


def shards(
    video,
    stereo_qk,
    stereo_v,
    stereo_out,
    temporal_qk,
    temporal_v,
    temporal_out,
    mlp_up,
    mix_kernel,
    mlp_down,
):
    width, channels = video.shape[-2:]
    frame_size, rows_size = lax.axis_size("frame"), lax.axis_size("rows")
    pairs = frame_size // 2
    owners = frame_size
    cols = width // owners
    window = round_up(cols + 2, 16)
    left = (window - cols) // 2
    frame, row = lax.axis_index("frame"), lax.axis_index("rows")
    pair, side = frame // 2, row % 2
    side_arg = side.astype(jnp.int32)[None]
    both = ("frame", "rows")
    slots = [(s, p) for s in range(2) for p in range(pairs)]

    def owner_at(s, p):
        return lax.rem(pair + p, pairs) * 2 + (side ^ s)

    def chip_moves(s, p):
        return [
            (
                f * rows_size + r,
                ((f // 2 + p) % pairs * 2 + f % 2) * rows_size + (r ^ s),
            )
            for f in range(frame_size)
            for r in range(rows_size)
        ]

    siblings = [(f, f ^ 1) for f in range(frame_size)]
    bands = rows_size // 2
    band_moves = []
    for slot in range(2):
        moves = []
        for r in range(rows_size):
            band = r // 2 + (1 if (r + slot) % 2 else -1)
            moves.append((r, band * 2 + r % 2 if 0 <= band < bands else r ^ 1))
        band_moves.append(moves)
    first_band, last_band = row // 2 == 0, row // 2 == bands - 1
    at_edge = (
        jnp.where(side == 0, last_band, first_band),
        jnp.where(side == 0, first_band, last_band),
    )
    edge_args = [edge.astype(jnp.int32)[None] for edge in at_edge]
    core_arg = (frame % 2).astype(jnp.int32)[None]
    sibling_video = lax.ppermute(video, "frame", siblings)
    windows, *weights = first_stereo(
        core_arg,
        video,
        owners,
        left,
        window,
        stereo_qk,
        stereo_v,
        stereo_out,
        temporal_qk,
        temporal_v,
        temporal_out,
    )
    sibling_windows = kernel_call(
        functools.partial(second_kernel, left, cols),
        "stereo",
        2_400_000_000,
        jax.ShapeDtypeStruct(windows.shape, windows.dtype),
        (core_arg,),
        sibling_video,
        *weights[:3],
    )
    pieces = {}
    for s, p in slots:
        index = owner_at(s, p)
        piece = jnp.stack(
            [
                lax.dynamic_index_in_dim(array, index, 0, keepdims=False)
                for array in (windows, sibling_windows)
            ]
        )
        if (s, p) != (0, 0):
            piece = lax.ppermute(piece, both, chip_moves(s, p))
        pieces[s, p] = piece
    shape = (pairs, 2, window, channels)
    sections, halos = [], []
    for s in range(2):
        section = kernel_call(
            functools.partial(temporal_kernel, pairs, -1 if s else 1),
            "temporal",
            1_000_000_000,
            jax.ShapeDtypeStruct(shape, jnp.bfloat16),
            (),
            *[pieces[s, p] for p in range(pairs)][:: -1 if s else 1],
            *weights[3:],
            after=sections[:],
        )
        sections.append(section)
        halos.append(lax.ppermute(section, "rows", band_moves[s]))
    partials = kernel_call(
        inner_kernel,
        "inner",
        4_000_000_000,
        [jax.ShapeDtypeStruct(shape, jnp.float32)] * 2,
        (side_arg,),
        *sections,
        mlp_up,
        mix_kernel,
        mlp_down,
    )
    results = {}
    earlier = []
    for s in (1, 0):
        own_out, sibling_out = kernel_call(
            functools.partial(outer_kernel, left, s),
            "outer",
            1_000_000_000,
            [jax.ShapeDtypeStruct((pairs, window, channels), jnp.bfloat16)] * 2,
            (side_arg, edge_args[1 - s]),
            partials[s],
            halos[1 - s],
            mlp_up,
            mix_kernel,
            mlp_down,
            after=earlier,
        )
        earlier = [own_out]
        other_out = lax.ppermute(sibling_out, "frame", siblings)
        first_view = jnp.where(frame % 2 == 0, own_out, other_out)
        second_view = jnp.where(frame % 2 == 0, other_out, own_out)
        for p in range(pairs):
            piece = jnp.stack([first_view[p, :cols], second_view[p, :cols]])
            if (s, p) != (0, 0):
                back = [(j, i) for i, j in chip_moves(s, p)]
                piece = lax.ppermute(piece, both, back)
            results[s, p] = piece
    strips = []
    for owner in range(owners):
        strip = results[slots[0]]
        for slot in slots[1:]:
            strip = jnp.where(owner_at(*slot) == owner, results[slot], strip)
        strips.append(strip)
    return jnp.concatenate(strips, axis=1).reshape(video.shape)


def solution(mesh):
    in_specs = (P(None, "frame", "rows", None, None), P(), P(), P(), P(), P(), P(), P(), P(), P())
    out_specs = P(None, "frame", "rows", None, None)
    return jax.shard_map(shards, mesh=mesh, in_specs=in_specs, out_specs=out_specs, check_vma=False)
```

```python
import functools

import jax
import jax.numpy as jnp
from jax import lax
from jax.experimental import pallas as pl
from jax.experimental.pallas import tpu as pltpu
from jax.sharding import PartitionSpec as P

HEADS = 8
HEAD_DIM = 32
SCALE_LOG2 = HEAD_DIM ** (-0.5) * 1.4426950408889634
VMEM_LIMIT = 40 * 1024 * 1024


def round_up(value, unit):
    return (value + unit - 1) // unit * unit


def layer_norm(widened):
    centred = widened - jnp.mean(widened, axis=-1, keepdims=True)
    variance = jnp.mean(centred * centred, axis=-1, keepdims=True)
    return (centred * lax.rsqrt(variance + 1e-05)).astype(jnp.bfloat16)


def dot_dims(lhs, rhs, lhs_dim, rhs_dim):
    return lax.dot_general(
        lhs, rhs, (((lhs_dim,), (rhs_dim,)), ((), ())), preferred_element_type=jnp.float32
    )


def stereo_rows(left, cols, rows, rows_other, qk_ref, v_ref, out_ref, windows_ref):
    width, channels = rows.shape
    normed = layer_norm(rows)
    normed_other = layer_norm(rows_other)
    queries = dot_dims(normed, qk_ref[:, :channels], 1, 0).astype(jnp.bfloat16)
    keys = dot_dims(normed_other, qk_ref[:, channels:], 1, 0).astype(jnp.bfloat16)
    values = dot_dims(normed_other, v_ref[...], 1, 0).astype(jnp.bfloat16)
    lane_head = lax.broadcasted_iota(jnp.int32, (width, 128), 1) // HEAD_DIM
    zero = jnp.zeros((), jnp.bfloat16)
    ones = jnp.ones((width, 128), jnp.bfloat16)
    owners, window, _ = windows_ref.shape
    tail = round_up((owners - 1) * cols + window, 8) - width
    groups = []
    for start in range(0, channels, 128):
        lanes = slice(start, start + 128)
        total = jnp.zeros((width, 128), jnp.float32)
        for head in range(128 // HEAD_DIM):
            mask = lane_head == head
            scores = dot_dims(queries[:, lanes], jnp.where(mask, keys[:, lanes], zero), 1, 1)
            top = jnp.max(scores, axis=1, keepdims=True)
            weights = jnp.exp2((scores - top) * SCALE_LOG2).astype(jnp.bfloat16)
            values_head = jnp.where(mask, values[:, lanes], zero)
            mixed = dot_dims(weights, jnp.concatenate([values_head, ones], axis=1), 1, 0)
            total = total + mixed[:, :128] * (1.0 / mixed[:, 128:])
        groups.append(total.astype(jnp.bfloat16))
    update = dot_dims(jnp.concatenate(groups, axis=1), out_ref[...], 1, 0)
    padded = jnp.concatenate([rows + update, jnp.zeros((tail, channels), jnp.float32)], axis=0)
    padded = pltpu.roll(padded, left, 0)
    for owner in range(owners):
        windows_ref[owner] = padded[owner * cols : owner * cols + window].astype(jnp.bfloat16)


def first_kernel(left, cols, core_ref, *refs):
    count = (len(refs) - 2) // 2
    sources, windows_ref = refs[:count], refs[count]
    targets, sems = (refs[-2], *refs[count + 1 : -2]), refs[-1]
    copies = [
        pltpu.make_async_copy(source, target, sems.at[index])
        for index, (source, target) in enumerate(zip(sources, targets))
    ]
    for copy in copies:
        copy.start()
    for copy in copies[:4]:
        copy.wait()
    second_kernel(left, cols, core_ref, *targets[:4], windows_ref)
    for copy in copies[4:]:
        copy.wait()


def second_kernel(left, cols, core_ref, video_ref, qk_ref, v_ref, out_ref, windows_ref):
    core = core_ref[0]
    width, channels = video_ref.shape[-2:]
    rows = video_ref[core].reshape(width, channels).astype(jnp.float32)
    rows_other = video_ref[1 - core].reshape(width, channels).astype(jnp.float32)
    stereo_rows(left, cols, rows, rows_other, qk_ref, v_ref, out_ref, windows_ref)


def first_stereo(core, video, owners, left, window, *weights):
    width, channels = video.shape[-2:]
    operands = [pltpu.with_memory_space_constraint(array, pltpu.HBM) for array in (video, *weights)]
    vmem = pl.BlockSpec(memory_space=pltpu.VMEM)
    return pl.pallas_call(
        functools.partial(first_kernel, left, width // owners),
        in_specs=[pl.BlockSpec(memory_space=pltpu.SMEM)]
        + [pl.BlockSpec(memory_space=pltpu.HBM)] * len(operands),
        out_specs=[vmem] * len(operands),
        out_shape=[jax.ShapeDtypeStruct((owners, window, channels), jnp.bfloat16)]
        + [jax.ShapeDtypeStruct(array.shape, array.dtype) for array in weights],
        scratch_shapes=[
            pltpu.VMEM(video.shape, video.dtype),
            pltpu.SemaphoreType.DMA((len(operands),)),
        ],
        compiler_params=pltpu.CompilerParams(vmem_limit_bytes=VMEM_LIMIT),
        cost_estimate=pl.CostEstimate(
            flops=2_400_000_000, bytes_accessed=2_000_000, transcendentals=2_000_000
        ),
        name="stereo",
    )(core, *operands)


def head_sum(product):
    channels, width = product.shape
    return jnp.sum(product.reshape(HEADS, HEAD_DIM, width), axis=1, keepdims=True)


def temporal_kernel(pairs, order, *refs):
    pieces, (qk_ref, v_ref, out_ref, section_ref) = refs[:pairs][::order], refs[pairs:]
    _, pair_size, window, channels = section_ref.shape
    frames = pairs * pair_size
    rows = jnp.concatenate(
        [piece[...].reshape(pair_size * window, channels) for piece in pieces], axis=0
    ).astype(jnp.float32)
    normed = layer_norm(rows)
    pairs_t = dot_dims(qk_ref[...], normed, 0, 1).astype(jnp.bfloat16)
    queries, keys = pairs_t[:channels], pairs_t[channels:]
    values = dot_dims(v_ref[...], normed, 0, 1).astype(jnp.bfloat16)
    attended = []
    for frame in range(frames):
        query = queries[:, frame * window : (frame + 1) * window].astype(jnp.float32)
        scores = [
            head_sum(query * keys[:, other * window : (other + 1) * window].astype(jnp.float32))
            for other in range(frames)
        ]
        top = functools.reduce(jnp.maximum, scores)
        weights = [jnp.exp2((score - top) * SCALE_LOG2) for score in scores]
        inverse = 1.0 / functools.reduce(jnp.add, weights)
        mixed = jnp.zeros((HEADS, HEAD_DIM, window), jnp.float32)
        for other in range(frames):
            value = values[:, other * window : (other + 1) * window].astype(jnp.float32)
            mixed = mixed + value.reshape(HEADS, HEAD_DIM, window) * (weights[other] * inverse)
        attended.append(mixed.reshape(channels, window).astype(jnp.bfloat16))
    update = dot_dims(jnp.concatenate(attended, axis=1), out_ref[...], 0, 0)
    section_ref[...] = (rows + update).astype(jnp.bfloat16).reshape(section_ref.shape)


def kernel_call(body, name, flops, out_shape, scalars, *operands, after=()):
    count = len(scalars) + len(operands)

    def ordered_body(*refs):
        body(*refs[:count], *refs[count + len(after) :])

    return pl.pallas_call(
        ordered_body,
        in_specs=[pl.BlockSpec(memory_space=pltpu.SMEM)] * len(scalars)
        + [pl.BlockSpec(memory_space=pltpu.VMEM)] * len(operands)
        + [pl.BlockSpec(memory_space=pl.ANY)] * len(after),
        out_specs=jax.tree.map(lambda _: pl.BlockSpec(memory_space=pltpu.VMEM), out_shape),
        out_shape=out_shape,
        compiler_params=pltpu.CompilerParams(vmem_limit_bytes=VMEM_LIMIT),
        cost_estimate=pl.CostEstimate(flops=flops, bytes_accessed=3_000_000, transcendentals=0),
        name=name,
    )(*scalars, *operands, *after)


def double_gelu(values):
    inner = values * (
        jnp.bfloat16(0.7978845608028654) + jnp.bfloat16(0.035677408136300125) * (values * values)
    )
    return values + values * jnp.tanh(inner)


def half_taps(mix_ref, tap, lanes):
    return mix_ref[tap, :, lanes] * jnp.bfloat16(0.5)


def mlp_mix(columns, window):
    columns = [column.astype(jnp.float32) for column in columns]
    return (
        pltpu.roll(columns[0], 1, 0) + columns[1] + pltpu.roll(columns[2], window - 1, 0)
    ).astype(jnp.bfloat16)


CHUNK = 256


def mlp_hidden(normed, up_ref, start):
    product = dot_dims(normed, up_ref[:, start : start + CHUNK], 1, 0)
    return double_gelu(product.astype(jnp.bfloat16))


def inner_kernel(side_ref, own_ref, next_ref, up_ref, mix_ref, down_ref, *partial_refs):
    pairs, pair_size, window, channels = own_ref.shape
    other_tap = (2 - 2 * side_ref[0], 2 * side_ref[0])
    for pair in range(pairs):
        for member in range(pair_size):
            rows = jnp.concatenate([own_ref[pair, member], next_ref[pair, member]], axis=0)
            rows = rows.astype(jnp.float32)
            normed = layer_norm(rows)
            total = rows
            for start in range(0, up_ref.shape[1], CHUNK):
                lanes = slice(start, start + CHUNK)
                hidden = mlp_hidden(normed, up_ref, start)
                lines = [hidden[:window], hidden[window:]]
                same = half_taps(mix_ref, 1, lanes)
                mixed = []
                for slot in range(2):
                    across = half_taps(mix_ref, other_tap[slot], lanes)
                    mixed.append(
                        mlp_mix(
                            [
                                lines[slot] * same[b][None] + lines[1 - slot] * across[b][None]
                                for b in range(3)
                            ],
                            window,
                        )
                    )
                total = total + dot_dims(jnp.concatenate(mixed, axis=0), down_ref[lanes], 1, 0)
            for slot in range(2):
                partial_refs[slot][pair, member] = total[slot * window : (slot + 1) * window]


def outer_kernel(
    left, slot, side_ref, edge_ref, partial_ref, halo_ref, up_ref, mix_ref, down_ref, out_ref
):
    pairs, pair_size, window, channels = partial_ref.shape
    tap = 2 * side_ref[0] if slot == 0 else 2 - 2 * side_ref[0]
    for pair in range(pairs):
        rows = halo_ref[pair].reshape(pair_size * window, channels).astype(jnp.float32)
        normed = layer_norm(jnp.where(edge_ref[0] == 1, jnp.zeros_like(rows), rows))
        total = partial_ref[pair].reshape(pair_size * window, channels)
        for start in range(0, up_ref.shape[1], CHUNK):
            lanes = slice(start, start + CHUNK)
            hidden = mlp_hidden(normed, up_ref, start)
            across = half_taps(mix_ref, tap, lanes)
            mixed = [
                mlp_mix(
                    [
                        hidden[member * window : (member + 1) * window] * across[b][None]
                        for b in range(3)
                    ],
                    window,
                )
                for member in range(pair_size)
            ]
            total = total + dot_dims(jnp.concatenate(mixed, axis=0), down_ref[lanes], 1, 0)
        for member in range(pair_size):
            shifted = pltpu.roll(total[member * window : (member + 1) * window], window - left, 0)
            out_ref[pair, member] = shifted.astype(jnp.bfloat16)


def shards(
    video,
    stereo_qk,
    stereo_v,
    stereo_out,
    temporal_qk,
    temporal_v,
    temporal_out,
    mlp_up,
    mix_kernel,
    mlp_down,
):
    width, channels = video.shape[-2:]
    frame_size, rows_size = lax.axis_size("frame"), lax.axis_size("rows")
    pairs = frame_size // 2
    owners = frame_size
    cols = width // owners
    window = round_up(cols + 2, 16)
    left = (window - cols) // 2
    frame, row = lax.axis_index("frame"), lax.axis_index("rows")
    pair, side = frame // 2, row % 2
    side_arg = side.astype(jnp.int32)[None]
    both = ("frame", "rows")
    slots = [(s, p) for s in range(2) for p in range(pairs)]

    def owner_at(s, p):
        return lax.rem(pair + p, pairs) * 2 + (side ^ s)

    def chip_moves(s, p):
        return [
            (
                f * rows_size + r,
                ((f // 2 + p) % pairs * 2 + f % 2) * rows_size + (r ^ s),
            )
            for f in range(frame_size)
            for r in range(rows_size)
        ]

    siblings = [(f, f ^ 1) for f in range(frame_size)]
    bands = rows_size // 2
    band_moves = []
    for slot in range(2):
        moves = []
        for r in range(rows_size):
            band = r // 2 + (1 if (r + slot) % 2 else -1)
            moves.append((r, band * 2 + r % 2 if 0 <= band < bands else r ^ 1))
        band_moves.append(moves)
    first_band, last_band = row // 2 == 0, row // 2 == bands - 1
    at_edge = (
        jnp.where(side == 0, last_band, first_band),
        jnp.where(side == 0, first_band, last_band),
    )
    edge_args = [edge.astype(jnp.int32)[None] for edge in at_edge]
    core_arg = (frame % 2).astype(jnp.int32)[None]
    sibling_video = lax.ppermute(video, "frame", siblings)
    windows, *weights = first_stereo(
        core_arg,
        video,
        owners,
        left,
        window,
        stereo_qk,
        stereo_v,
        stereo_out,
        temporal_qk,
        temporal_v,
        temporal_out,
    )
    sibling_windows = kernel_call(
        functools.partial(second_kernel, left, cols),
        "stereo",
        2_400_000_000,
        jax.ShapeDtypeStruct(windows.shape, windows.dtype),
        (core_arg,),
        sibling_video,
        *weights[:3],
    )
    pieces = {}
    for s, p in slots:
        index = owner_at(s, p)
        piece = jnp.stack(
            [
                lax.dynamic_index_in_dim(array, index, 0, keepdims=False)
                for array in (windows, sibling_windows)
            ]
        )
        if (s, p) != (0, 0):
            piece = lax.ppermute(piece, both, chip_moves(s, p))
        pieces[s, p] = piece
    shape = (pairs, 2, window, channels)
    sections, halos = [], []
    for s in range(2):
        section = kernel_call(
            functools.partial(temporal_kernel, pairs, -1 if s else 1),
            "temporal",
            1_000_000_000,
            jax.ShapeDtypeStruct(shape, jnp.bfloat16),
            (),
            *[pieces[s, p] for p in range(pairs)][:: -1 if s else 1],
            *weights[3:],
            after=sections[:],
        )
        sections.append(section)
        halos.append(lax.ppermute(section, "rows", band_moves[s]))
    partials = kernel_call(
        inner_kernel,
        "inner",
        4_000_000_000,
        [jax.ShapeDtypeStruct(shape, jnp.float32)] * 2,
        (side_arg,),
        *sections,
        mlp_up,
        mix_kernel,
        mlp_down,
    )
    results, crossed, earlier = {}, {}, []
    for s in (1, 0):
        finished = kernel_call(
            functools.partial(outer_kernel, left, s),
            "outer",
            1_000_000_000,
            jax.ShapeDtypeStruct(shape, jnp.bfloat16),
            (side_arg, edge_args[1 - s]),
            partials[s],
            halos[1 - s],
            mlp_up,
            mix_kernel,
            mlp_down,
            after=earlier,
        )
        earlier = [finished]
        for p in range(pairs):
            piece = finished[p, :, :cols]
            if (s, p) != (0, 0):
                back = [(j, i) for i, j in chip_moves(s, p)]
                piece = lax.ppermute(piece, both, back)
            results[s, p] = piece
    for group in (slots[:1] + slots[pairs:pairs + 1], slots[1:pairs] + slots[pairs + 1:]):
        sent = jnp.stack([results[slot][1] for slot in group])
        received = lax.ppermute(sent, "frame", siblings)
        for index, slot in enumerate(group):
            crossed[slot] = received[index]
    strips = [[], []]
    for owner in range(owners):
        own, other = results[slots[0]][0], crossed[slots[0]]
        for slot in slots[1:]:
            here = owner_at(*slot) == owner
            own = jnp.where(here, results[slot][0], own)
            other = jnp.where(here, crossed[slot], other)
        strips[0].append(jnp.where(frame % 2 == 0, own, other))
        strips[1].append(jnp.where(frame % 2 == 0, other, own))
    return jnp.stack([jnp.concatenate(strip) for strip in strips]).reshape(video.shape)


def solution(mesh):
    in_specs = (P(None, "frame", "rows", None, None), P(), P(), P(), P(), P(), P(), P(), P(), P())
    out_specs = P(None, "frame", "rows", None, None)
    return jax.shard_map(shards, mesh=mesh, in_specs=in_specs, out_specs=out_specs, check_vma=False)
```

```python
import functools

import jax
import jax.numpy as jnp
from jax import lax
from jax.experimental import pallas as pl
from jax.experimental.pallas import tpu as pltpu
from jax.sharding import PartitionSpec as P

HEADS = 8
HEAD_DIM = 32
SCALE_LOG2 = HEAD_DIM ** (-0.5) * 1.4426950408889634
VMEM_LIMIT = 40 * 1024 * 1024


def round_up(value, unit):
    return (value + unit - 1) // unit * unit


def layer_norm(widened):
    centred = widened - jnp.mean(widened, axis=-1, keepdims=True)
    variance = jnp.mean(centred * centred, axis=-1, keepdims=True)
    return (centred * lax.rsqrt(variance + 1e-05)).astype(jnp.bfloat16)


def dot_dims(lhs, rhs, lhs_dim, rhs_dim):
    return lax.dot_general(
        lhs, rhs, (((lhs_dim,), (rhs_dim,)), ((), ())), preferred_element_type=jnp.float32
    )


def stereo_rows(left, cols, rows, rows_other, qk_ref, v_ref, out_ref, windows_ref):
    width, channels = rows.shape
    normed = layer_norm(rows)
    normed_other = layer_norm(rows_other)
    queries = dot_dims(normed, qk_ref[:, :channels], 1, 0).astype(jnp.bfloat16)
    keys = dot_dims(normed_other, qk_ref[:, channels:], 1, 0).astype(jnp.bfloat16)
    values = dot_dims(normed_other, v_ref[...], 1, 0).astype(jnp.bfloat16)
    lane_head = lax.broadcasted_iota(jnp.int32, (width, 128), 1) // HEAD_DIM
    zero = jnp.zeros((), jnp.bfloat16)
    ones = jnp.ones((width, 128), jnp.bfloat16)
    owners, window, _ = windows_ref.shape
    tail = round_up((owners - 1) * cols + window, 8) - width
    groups = []
    for start in range(0, channels, 128):
        lanes = slice(start, start + 128)
        total = jnp.zeros((width, 128), jnp.float32)
        for head in range(128 // HEAD_DIM):
            mask = lane_head == head
            scores = dot_dims(queries[:, lanes], jnp.where(mask, keys[:, lanes], zero), 1, 1)
            top = jnp.max(scores, axis=1, keepdims=True)
            weights = jnp.exp2((scores - top) * SCALE_LOG2).astype(jnp.bfloat16)
            values_head = jnp.where(mask, values[:, lanes], zero)
            mixed = dot_dims(weights, jnp.concatenate([values_head, ones], axis=1), 1, 0)
            total = total + mixed[:, :128] * (1.0 / mixed[:, 128:])
        groups.append(total.astype(jnp.bfloat16))
    update = dot_dims(jnp.concatenate(groups, axis=1), out_ref[...], 1, 0)
    padded = jnp.concatenate([rows + update, jnp.zeros((tail, channels), jnp.float32)], axis=0)
    padded = pltpu.roll(padded, left, 0)
    for owner in range(owners):
        windows_ref[owner] = padded[owner * cols : owner * cols + window].astype(jnp.bfloat16)


def first_kernel(left, cols, core_ref, *refs):
    count = (len(refs) - 2) // 2
    sources, windows_ref = refs[:count], refs[count]
    targets, sems = (refs[-2], *refs[count + 1 : -2]), refs[-1]
    copies = [
        pltpu.make_async_copy(source, target, sems.at[index])
        for index, (source, target) in enumerate(zip(sources, targets))
    ]
    for copy in copies:
        copy.start()
    for copy in copies[:4]:
        copy.wait()
    second_kernel(left, cols, core_ref, *targets[:4], windows_ref)
    for copy in copies[4:]:
        copy.wait()


def second_kernel(left, cols, core_ref, video_ref, qk_ref, v_ref, out_ref, windows_ref):
    core = core_ref[0]
    width, channels = video_ref.shape[-2:]
    rows = video_ref[core].reshape(width, channels).astype(jnp.float32)
    rows_other = video_ref[1 - core].reshape(width, channels).astype(jnp.float32)
    stereo_rows(left, cols, rows, rows_other, qk_ref, v_ref, out_ref, windows_ref)


def first_stereo(core, video, owners, left, window, *weights):
    width, channels = video.shape[-2:]
    operands = [pltpu.with_memory_space_constraint(array, pltpu.HBM) for array in (video, *weights)]
    vmem = pl.BlockSpec(memory_space=pltpu.VMEM)
    return pl.pallas_call(
        functools.partial(first_kernel, left, width // owners),
        in_specs=[pl.BlockSpec(memory_space=pltpu.SMEM)]
        + [pl.BlockSpec(memory_space=pltpu.HBM)] * len(operands),
        out_specs=[vmem] * len(operands),
        out_shape=[jax.ShapeDtypeStruct((owners, window, channels), jnp.bfloat16)]
        + [jax.ShapeDtypeStruct(array.shape, array.dtype) for array in weights],
        scratch_shapes=[
            pltpu.VMEM(video.shape, video.dtype),
            pltpu.SemaphoreType.DMA((len(operands),)),
        ],
        compiler_params=pltpu.CompilerParams(vmem_limit_bytes=VMEM_LIMIT),
        cost_estimate=pl.CostEstimate(
            flops=2_400_000_000, bytes_accessed=2_000_000, transcendentals=2_000_000
        ),
        name="stereo",
    )(core, *operands)


def head_sum(product):
    channels, width = product.shape
    return jnp.sum(product.reshape(HEADS, HEAD_DIM, width), axis=1, keepdims=True)


def temporal_kernel(pairs, order, *refs):
    pieces, (qk_ref, v_ref, out_ref, section_ref) = refs[:pairs][::order], refs[pairs:]
    _, pair_size, window, channels = section_ref.shape
    frames = pairs * pair_size
    rows = jnp.concatenate(
        [piece[...].reshape(pair_size * window, channels) for piece in pieces], axis=0
    ).astype(jnp.float32)
    normed = layer_norm(rows)
    pairs_t = dot_dims(qk_ref[...], normed, 0, 1).astype(jnp.bfloat16)
    queries, keys = pairs_t[:channels], pairs_t[channels:]
    values = dot_dims(v_ref[...], normed, 0, 1).astype(jnp.bfloat16)
    attended = []
    for frame in range(frames):
        query = queries[:, frame * window : (frame + 1) * window].astype(jnp.float32)
        scores = [
            head_sum(query * keys[:, other * window : (other + 1) * window].astype(jnp.float32))
            for other in range(frames)
        ]
        top = functools.reduce(jnp.maximum, scores)
        weights = [jnp.exp2((score - top) * SCALE_LOG2) for score in scores]
        inverse = 1.0 / functools.reduce(jnp.add, weights)
        mixed = jnp.zeros((HEADS, HEAD_DIM, window), jnp.float32)
        for other in range(frames):
            value = values[:, other * window : (other + 1) * window].astype(jnp.float32)
            mixed = mixed + value.reshape(HEADS, HEAD_DIM, window) * (weights[other] * inverse)
        attended.append(mixed.reshape(channels, window).astype(jnp.bfloat16))
    update = dot_dims(jnp.concatenate(attended, axis=1), out_ref[...], 0, 0)
    section_ref[...] = (rows + update).astype(jnp.bfloat16).reshape(section_ref.shape)


def kernel_call(body, name, flops, out_shape, scalars, *operands, after=()):
    count = len(scalars) + len(operands)

    def ordered_body(*refs):
        body(*refs[:count], *refs[count + len(after) :])

    return pl.pallas_call(
        ordered_body,
        in_specs=[pl.BlockSpec(memory_space=pltpu.SMEM)] * len(scalars)
        + [pl.BlockSpec(memory_space=pltpu.VMEM)] * len(operands)
        + [pl.BlockSpec(memory_space=pl.ANY)] * len(after),
        out_specs=jax.tree.map(lambda _: pl.BlockSpec(memory_space=pltpu.VMEM), out_shape),
        out_shape=out_shape,
        compiler_params=pltpu.CompilerParams(vmem_limit_bytes=VMEM_LIMIT),
        cost_estimate=pl.CostEstimate(flops=flops, bytes_accessed=3_000_000, transcendentals=0),
        name=name,
    )(*scalars, *operands, *after)


def double_gelu(values):
    inner = values * (
        jnp.bfloat16(0.7978845608028654) + jnp.bfloat16(0.035677408136300125) * (values * values)
    )
    return values + values * jnp.tanh(inner)


def half_taps(mix_ref, tap, lanes):
    return mix_ref[tap, :, lanes] * jnp.bfloat16(0.5)


def mlp_mix(columns, window):
    columns = [column.astype(jnp.float32) for column in columns]
    return (
        pltpu.roll(columns[0], 1, 0) + columns[1] + pltpu.roll(columns[2], window - 1, 0)
    ).astype(jnp.bfloat16)


CHUNK = 256


def mlp_hidden(normed, up_ref, start):
    product = dot_dims(normed, up_ref[:, start : start + CHUNK], 1, 0)
    return double_gelu(product.astype(jnp.bfloat16))


def inner_kernel(side_ref, own_ref, next_ref, up_ref, mix_ref, down_ref, *partial_refs):
    pairs, pair_size, window, channels = own_ref.shape
    other_tap = (2 - 2 * side_ref[0], 2 * side_ref[0])
    for pair in range(pairs):
        for member in range(pair_size):
            rows = jnp.concatenate([own_ref[pair, member], next_ref[pair, member]], axis=0)
            rows = rows.astype(jnp.float32)
            normed = layer_norm(rows)
            total = rows
            for start in range(0, up_ref.shape[1], CHUNK):
                lanes = slice(start, start + CHUNK)
                hidden = mlp_hidden(normed, up_ref, start)
                lines = [hidden[:window], hidden[window:]]
                same = half_taps(mix_ref, 1, lanes)
                mixed = []
                for slot in range(2):
                    across = half_taps(mix_ref, other_tap[slot], lanes)
                    mixed.append(
                        mlp_mix(
                            [
                                lines[slot] * same[b][None] + lines[1 - slot] * across[b][None]
                                for b in range(3)
                            ],
                            window,
                        )
                    )
                total = total + dot_dims(jnp.concatenate(mixed, axis=0), down_ref[lanes], 1, 0)
            for slot in range(2):
                partial_refs[slot][pair, member] = total[slot * window : (slot + 1) * window]


def outer_kernel(
    left, slot, chosen, side_ref, edge_ref, partial_ref, halo_ref, up_ref, mix_ref, down_ref, out_ref
):
    _, pair_size, window, channels = partial_ref.shape
    tap = 2 * side_ref[0] if slot == 0 else 2 - 2 * side_ref[0]
    for place, pair in enumerate(chosen):
        rows = halo_ref[pair].reshape(pair_size * window, channels).astype(jnp.float32)
        normed = layer_norm(jnp.where(edge_ref[0] == 1, jnp.zeros_like(rows), rows))
        total = partial_ref[pair].reshape(pair_size * window, channels)
        for start in range(0, up_ref.shape[1], CHUNK):
            lanes = slice(start, start + CHUNK)
            hidden = mlp_hidden(normed, up_ref, start)
            across = half_taps(mix_ref, tap, lanes)
            mixed = [
                mlp_mix(
                    [
                        hidden[member * window : (member + 1) * window] * across[b][None]
                        for b in range(3)
                    ],
                    window,
                )
                for member in range(pair_size)
            ]
            total = total + dot_dims(jnp.concatenate(mixed, axis=0), down_ref[lanes], 1, 0)
        for member in range(pair_size):
            shifted = pltpu.roll(total[member * window : (member + 1) * window], window - left, 0)
            out_ref[place, member] = shifted.astype(jnp.bfloat16)


def shards(
    video,
    stereo_qk,
    stereo_v,
    stereo_out,
    temporal_qk,
    temporal_v,
    temporal_out,
    mlp_up,
    mix_kernel,
    mlp_down,
):
    width, channels = video.shape[-2:]
    frame_size, rows_size = lax.axis_size("frame"), lax.axis_size("rows")
    pairs = frame_size // 2
    owners = frame_size
    cols = width // owners
    window = round_up(cols + 2, 16)
    left = (window - cols) // 2
    frame, row = lax.axis_index("frame"), lax.axis_index("rows")
    pair, side = frame // 2, row % 2
    side_arg = side.astype(jnp.int32)[None]
    both = ("frame", "rows")
    slots = [(s, p) for s in range(2) for p in range(pairs)]

    def owner_at(s, p):
        return lax.rem(pair + p, pairs) * 2 + (side ^ s)

    def chip_moves(s, p):
        return [
            (
                f * rows_size + r,
                ((f // 2 + p) % pairs * 2 + f % 2) * rows_size + (r ^ s),
            )
            for f in range(frame_size)
            for r in range(rows_size)
        ]

    siblings = [(f, f ^ 1) for f in range(frame_size)]
    bands = rows_size // 2
    band_moves = []
    for slot in range(2):
        moves = []
        for r in range(rows_size):
            band = r // 2 + (1 if (r + slot) % 2 else -1)
            moves.append((r, band * 2 + r % 2 if 0 <= band < bands else r ^ 1))
        band_moves.append(moves)
    first_band, last_band = row // 2 == 0, row // 2 == bands - 1
    at_edge = (
        jnp.where(side == 0, last_band, first_band),
        jnp.where(side == 0, first_band, last_band),
    )
    edge_args = [edge.astype(jnp.int32)[None] for edge in at_edge]
    core_arg = (frame % 2).astype(jnp.int32)[None]
    sibling_video = lax.ppermute(video, "frame", siblings)
    windows, *weights = first_stereo(
        core_arg,
        video,
        owners,
        left,
        window,
        stereo_qk,
        stereo_v,
        stereo_out,
        temporal_qk,
        temporal_v,
        temporal_out,
    )
    sibling_windows = kernel_call(
        functools.partial(second_kernel, left, cols),
        "stereo",
        2_400_000_000,
        jax.ShapeDtypeStruct(windows.shape, windows.dtype),
        (core_arg,),
        sibling_video,
        *weights[:3],
    )
    pieces = {}
    for s, p in slots:
        index = owner_at(s, p)
        piece = jnp.stack(
            [
                lax.dynamic_index_in_dim(array, index, 0, keepdims=False)
                for array in (windows, sibling_windows)
            ]
        )
        if (s, p) != (0, 0):
            piece = lax.ppermute(piece, both, chip_moves(s, p))
        pieces[s, p] = piece
    shape = (pairs, 2, window, channels)
    sections, halos = [], []
    for s in range(2):
        section = kernel_call(
            functools.partial(temporal_kernel, pairs, -1 if s else 1),
            "temporal",
            1_000_000_000,
            jax.ShapeDtypeStruct(shape, jnp.bfloat16),
            (),
            *[pieces[s, p] for p in range(pairs)][:: -1 if s else 1],
            *weights[3:],
            after=sections[:],
        )
        sections.append(section)
        halos.append(lax.ppermute(section, "rows", band_moves[s]))
    partials = kernel_call(
        inner_kernel,
        "inner",
        4_000_000_000,
        [jax.ShapeDtypeStruct(shape, jnp.float32)] * 2,
        (side_arg,),
        *sections,
        mlp_up,
        mix_kernel,
        mlp_down,
    )
    results, crossed, earlier = {}, {}, []
    calls = [(1, list(range(pairs))), (0, list(range(1, pairs))), (0, [0])]
    for s, chosen in calls:
        finished = kernel_call(
            functools.partial(outer_kernel, left, s, chosen),
            "outer",
            500_000_000 * len(chosen),
            jax.ShapeDtypeStruct((len(chosen),) + shape[1:], jnp.bfloat16),
            (side_arg, edge_args[1 - s]),
            partials[s],
            halos[1 - s],
            mlp_up,
            mix_kernel,
            mlp_down,
            after=earlier,
        )
        earlier = [finished]
        for place, p in enumerate(chosen):
            piece = finished[place, :, :cols]
            if (s, p) != (0, 0):
                back = [(j, i) for i, j in chip_moves(s, p)]
                piece = lax.ppermute(piece, both, back)
            results[s, p] = piece
    for group in (slots[:1] + slots[pairs:pairs + 1], slots[1:pairs] + slots[pairs + 1:]):
        sent = jnp.stack([results[slot][1] for slot in group])
        received = lax.ppermute(sent, "frame", siblings)
        for index, slot in enumerate(group):
            crossed[slot] = received[index]
    strips = [[], []]
    for owner in range(owners):
        own, other = results[slots[0]][0], crossed[slots[0]]
        for slot in slots[1:]:
            here = owner_at(*slot) == owner
            own = jnp.where(here, results[slot][0], own)
            other = jnp.where(here, crossed[slot], other)
        strips[0].append(jnp.where(frame % 2 == 0, own, other))
        strips[1].append(jnp.where(frame % 2 == 0, other, own))
    return jnp.stack([jnp.concatenate(strip) for strip in strips]).reshape(video.shape)


def solution(mesh):
    in_specs = (P(None, "frame", "rows", None, None), P(), P(), P(), P(), P(), P(), P(), P(), P())
    out_specs = P(None, "frame", "rows", None, None)
    return jax.shard_map(shards, mesh=mesh, in_specs=in_specs, out_specs=out_specs, check_vma=False)
```

```python
import functools

import jax
import jax.numpy as jnp
from jax import lax
from jax.experimental import pallas as pl
from jax.experimental.pallas import tpu as pltpu
from jax.sharding import PartitionSpec as P

HEADS = 8
HEAD_DIM = 32
SCALE_LOG2 = HEAD_DIM ** (-0.5) * 1.4426950408889634
VMEM_LIMIT = 40 * 1024 * 1024


def round_up(value, unit):
    return (value + unit - 1) // unit * unit


def layer_norm(widened):
    centred = widened - jnp.mean(widened, axis=-1, keepdims=True)
    variance = jnp.mean(centred * centred, axis=-1, keepdims=True)
    return (centred * lax.rsqrt(variance + 1e-05)).astype(jnp.bfloat16)


def dot_dims(lhs, rhs, lhs_dim, rhs_dim):
    return lax.dot_general(
        lhs, rhs, (((lhs_dim,), (rhs_dim,)), ((), ())), preferred_element_type=jnp.float32
    )


def stereo_rows(left, cols, rows, rows_other, qk_ref, v_ref, out_ref, windows_ref):
    width, channels = rows.shape
    normed = layer_norm(rows)
    normed_other = layer_norm(rows_other)
    queries = dot_dims(normed, qk_ref[:, :channels], 1, 0).astype(jnp.bfloat16)
    keys = dot_dims(normed_other, qk_ref[:, channels:], 1, 0).astype(jnp.bfloat16)
    values = dot_dims(normed_other, v_ref[...], 1, 0).astype(jnp.bfloat16)
    lane_head = lax.broadcasted_iota(jnp.int32, (width, 128), 1) // HEAD_DIM
    zero = jnp.zeros((), jnp.bfloat16)
    ones = jnp.ones((width, 128), jnp.bfloat16)
    owners, window, _ = windows_ref.shape
    tail = round_up((owners - 1) * cols + window, 8) - width
    groups = []
    for start in range(0, channels, 128):
        lanes = slice(start, start + 128)
        total = jnp.zeros((width, 128), jnp.float32)
        for head in range(128 // HEAD_DIM):
            mask = lane_head == head
            scores = dot_dims(queries[:, lanes], jnp.where(mask, keys[:, lanes], zero), 1, 1)
            top = jnp.max(scores, axis=1, keepdims=True)
            weights = jnp.exp2((scores - top) * SCALE_LOG2).astype(jnp.bfloat16)
            values_head = jnp.where(mask, values[:, lanes], zero)
            mixed = dot_dims(weights, jnp.concatenate([values_head, ones], axis=1), 1, 0)
            total = total + mixed[:, :128] * (1.0 / mixed[:, 128:])
        groups.append(total.astype(jnp.bfloat16))
    update = dot_dims(jnp.concatenate(groups, axis=1), out_ref[...], 1, 0)
    padded = jnp.concatenate([rows + update, jnp.zeros((tail, channels), jnp.float32)], axis=0)
    padded = pltpu.roll(padded, left, 0)
    for owner in range(owners):
        windows_ref[owner] = padded[owner * cols : owner * cols + window].astype(jnp.bfloat16)


def first_kernel(left, cols, core_ref, *refs):
    count = (len(refs) - 2) // 2
    sources, windows_ref = refs[:count], refs[count]
    targets, sems = (refs[-2], *refs[count + 1 : -2]), refs[-1]
    copies = [
        pltpu.make_async_copy(source, target, sems.at[index])
        for index, (source, target) in enumerate(zip(sources, targets))
    ]
    for copy in copies:
        copy.start()
    for copy in copies[:4]:
        copy.wait()
    second_kernel(left, cols, core_ref, *targets[:4], windows_ref)
    for copy in copies[4:]:
        copy.wait()


def second_kernel(left, cols, core_ref, video_ref, qk_ref, v_ref, out_ref, windows_ref):
    core = core_ref[0]
    width, channels = video_ref.shape[-2:]
    rows = video_ref[core].reshape(width, channels).astype(jnp.float32)
    rows_other = video_ref[1 - core].reshape(width, channels).astype(jnp.float32)
    stereo_rows(left, cols, rows, rows_other, qk_ref, v_ref, out_ref, windows_ref)


def first_stereo(core, video, owners, left, window, *weights):
    width, channels = video.shape[-2:]
    operands = [pltpu.with_memory_space_constraint(array, pltpu.HBM) for array in (video, *weights)]
    vmem = pl.BlockSpec(memory_space=pltpu.VMEM)
    return pl.pallas_call(
        functools.partial(first_kernel, left, width // owners),
        in_specs=[pl.BlockSpec(memory_space=pltpu.SMEM)]
        + [pl.BlockSpec(memory_space=pltpu.HBM)] * len(operands),
        out_specs=[vmem] * len(operands),
        out_shape=[jax.ShapeDtypeStruct((owners, window, channels), jnp.bfloat16)]
        + [jax.ShapeDtypeStruct(array.shape, array.dtype) for array in weights],
        scratch_shapes=[
            pltpu.VMEM(video.shape, video.dtype),
            pltpu.SemaphoreType.DMA((len(operands),)),
        ],
        compiler_params=pltpu.CompilerParams(vmem_limit_bytes=VMEM_LIMIT),
        cost_estimate=pl.CostEstimate(
            flops=2_400_000_000, bytes_accessed=2_000_000, transcendentals=2_000_000
        ),
        name="stereo",
    )(core, *operands)


def head_sum(product):
    channels, width = product.shape
    return jnp.sum(product.reshape(HEADS, HEAD_DIM, width), axis=1, keepdims=True)


def temporal_kernel(pairs, order, *refs):
    pieces, (qk_ref, v_ref, out_ref, section_ref) = refs[:pairs][::order], refs[pairs:]
    _, pair_size, window, channels = section_ref.shape
    frames = pairs * pair_size
    rows = jnp.concatenate(
        [piece[...].reshape(pair_size * window, channels) for piece in pieces], axis=0
    ).astype(jnp.float32)
    normed = layer_norm(rows)
    pairs_t = dot_dims(qk_ref[...], normed, 0, 1).astype(jnp.bfloat16)
    queries, keys = pairs_t[:channels], pairs_t[channels:]
    values = dot_dims(v_ref[...], normed, 0, 1).astype(jnp.bfloat16)
    attended = []
    for frame in range(frames):
        query = queries[:, frame * window : (frame + 1) * window].astype(jnp.float32)
        scores = [
            head_sum(query * keys[:, other * window : (other + 1) * window].astype(jnp.float32))
            for other in range(frames)
        ]
        top = functools.reduce(jnp.maximum, scores)
        weights = [jnp.exp2((score - top) * SCALE_LOG2) for score in scores]
        inverse = 1.0 / functools.reduce(jnp.add, weights)
        mixed = jnp.zeros((HEADS, HEAD_DIM, window), jnp.float32)
        for other in range(frames):
            value = values[:, other * window : (other + 1) * window].astype(jnp.float32)
            mixed = mixed + value.reshape(HEADS, HEAD_DIM, window) * (weights[other] * inverse)
        attended.append(mixed.reshape(channels, window).astype(jnp.bfloat16))
    update = dot_dims(jnp.concatenate(attended, axis=1), out_ref[...], 0, 0)
    section_ref[...] = (rows + update).astype(jnp.bfloat16).reshape(section_ref.shape)


def kernel_call(body, name, flops, out_shape, scalars, *operands, after=()):
    count = len(scalars) + len(operands)

    def ordered_body(*refs):
        body(*refs[:count], *refs[count + len(after) :])

    return pl.pallas_call(
        ordered_body,
        in_specs=[pl.BlockSpec(memory_space=pltpu.SMEM)] * len(scalars)
        + [pl.BlockSpec(memory_space=pltpu.VMEM)] * len(operands)
        + [pl.BlockSpec(memory_space=pl.ANY)] * len(after),
        out_specs=jax.tree.map(lambda _: pl.BlockSpec(memory_space=pltpu.VMEM), out_shape),
        out_shape=out_shape,
        compiler_params=pltpu.CompilerParams(vmem_limit_bytes=VMEM_LIMIT),
        cost_estimate=pl.CostEstimate(flops=flops, bytes_accessed=3_000_000, transcendentals=0),
        name=name,
    )(*scalars, *operands, *after)


def double_gelu(values):
    inner = values * (
        jnp.bfloat16(0.7978845608028654) + jnp.bfloat16(0.035677408136300125) * (values * values)
    )
    return values + values * jnp.tanh(inner)


def half_taps(mix_ref, tap, lanes):
    return mix_ref[tap, :, lanes] * jnp.bfloat16(0.5)


def mlp_mix(columns, window):
    columns = [column.astype(jnp.float32) for column in columns]
    return (
        pltpu.roll(columns[0], 1, 0) + columns[1] + pltpu.roll(columns[2], window - 1, 0)
    ).astype(jnp.bfloat16)


CHUNK = 256


def mlp_hidden(normed, up_ref, start):
    product = dot_dims(normed, up_ref[:, start : start + CHUNK], 1, 0)
    return double_gelu(product.astype(jnp.bfloat16))


def inner_kernel(side_ref, own_ref, next_ref, up_ref, mix_ref, down_ref, *partial_refs):
    pairs, pair_size, window, channels = own_ref.shape
    other_tap = (2 - 2 * side_ref[0], 2 * side_ref[0])
    for pair in range(pairs):
        for member in range(pair_size):
            rows = jnp.concatenate([own_ref[pair, member], next_ref[pair, member]], axis=0)
            rows = rows.astype(jnp.float32)
            normed = layer_norm(rows)
            total = rows
            for start in range(0, up_ref.shape[1], CHUNK):
                lanes = slice(start, start + CHUNK)
                hidden = mlp_hidden(normed, up_ref, start)
                lines = [hidden[:window], hidden[window:]]
                same = half_taps(mix_ref, 1, lanes)
                mixed = []
                for slot in range(2):
                    across = half_taps(mix_ref, other_tap[slot], lanes)
                    mixed.append(
                        mlp_mix(
                            [
                                lines[slot] * same[b][None] + lines[1 - slot] * across[b][None]
                                for b in range(3)
                            ],
                            window,
                        )
                    )
                total = total + dot_dims(jnp.concatenate(mixed, axis=0), down_ref[lanes], 1, 0)
            for slot in range(2):
                partial_refs[slot][pair, member] = total[slot * window : (slot + 1) * window]


def outer_kernel(
    left, slot, chosen, side_ref, edge_ref, partial_ref, halo_ref, up_ref, mix_ref, down_ref, out_ref
):
    _, pair_size, window, channels = partial_ref.shape
    tap = 2 * side_ref[0] if slot == 0 else 2 - 2 * side_ref[0]
    for place, pair in enumerate(chosen):
        rows = halo_ref[pair].reshape(pair_size * window, channels).astype(jnp.float32)
        normed = layer_norm(jnp.where(edge_ref[0] == 1, jnp.zeros_like(rows), rows))
        total = partial_ref[pair].reshape(pair_size * window, channels)
        for start in range(0, up_ref.shape[1], CHUNK):
            lanes = slice(start, start + CHUNK)
            hidden = mlp_hidden(normed, up_ref, start)
            across = half_taps(mix_ref, tap, lanes)
            mixed = [
                mlp_mix(
                    [
                        hidden[member * window : (member + 1) * window] * across[b][None]
                        for b in range(3)
                    ],
                    window,
                )
                for member in range(pair_size)
            ]
            total = total + dot_dims(jnp.concatenate(mixed, axis=0), down_ref[lanes], 1, 0)
        for member in range(pair_size):
            shifted = pltpu.roll(total[member * window : (member + 1) * window], window - left, 0)
            out_ref[place, member] = shifted.astype(jnp.bfloat16)


def shards(
    video,
    stereo_qk,
    stereo_v,
    stereo_out,
    temporal_qk,
    temporal_v,
    temporal_out,
    mlp_up,
    mix_kernel,
    mlp_down,
):
    width, channels = video.shape[-2:]
    frame_size, rows_size = lax.axis_size("frame"), lax.axis_size("rows")
    pairs = frame_size // 2
    owners = frame_size
    cols = width // owners
    window = round_up(cols + 2, 16)
    left = (window - cols) // 2
    frame, row = lax.axis_index("frame"), lax.axis_index("rows")
    pair, side = frame // 2, row % 2
    side_arg = side.astype(jnp.int32)[None]
    both = ("frame", "rows")
    slots = [(s, p) for s in range(2) for p in range(pairs)]

    def owner_at(s, p):
        return lax.rem(pair + p, pairs) * 2 + (side ^ s)

    def chip_moves(s, p):
        return [
            (
                f * rows_size + r,
                ((f // 2 + p) % pairs * 2 + f % 2) * rows_size + (r ^ s),
            )
            for f in range(frame_size)
            for r in range(rows_size)
        ]

    siblings = [(f, f ^ 1) for f in range(frame_size)]
    bands = rows_size // 2
    band_moves = []
    for slot in range(2):
        moves = []
        for r in range(rows_size):
            band = r // 2 + (1 if (r + slot) % 2 else -1)
            moves.append((r, band * 2 + r % 2 if 0 <= band < bands else r ^ 1))
        band_moves.append(moves)
    first_band, last_band = row // 2 == 0, row // 2 == bands - 1
    at_edge = (
        jnp.where(side == 0, last_band, first_band),
        jnp.where(side == 0, first_band, last_band),
    )
    edge_args = [edge.astype(jnp.int32)[None] for edge in at_edge]
    core_arg = (frame % 2).astype(jnp.int32)[None]
    sibling_video = lax.ppermute(video, "frame", siblings)
    windows, *weights = first_stereo(
        core_arg,
        video,
        owners,
        left,
        window,
        stereo_qk,
        stereo_v,
        stereo_out,
        temporal_qk,
        temporal_v,
        temporal_out,
    )
    sibling_windows = kernel_call(
        functools.partial(second_kernel, left, cols),
        "stereo",
        2_400_000_000,
        jax.ShapeDtypeStruct(windows.shape, windows.dtype),
        (core_arg,),
        sibling_video,
        *weights[:3],
    )
    pieces = {}
    for s, p in slots:
        index = owner_at(s, p)
        piece = jnp.stack(
            [
                lax.dynamic_index_in_dim(array, index, 0, keepdims=False)
                for array in (windows, sibling_windows)
            ]
        )
        if (s, p) != (0, 0):
            piece = lax.ppermute(piece, both, chip_moves(s, p))
        pieces[s, p] = piece
    shape = (pairs, 2, window, channels)
    sections, halos = [], []
    for s in range(2):
        section = kernel_call(
            functools.partial(temporal_kernel, pairs, 1),
            "temporal",
            1_000_000_000,
            jax.ShapeDtypeStruct(shape, jnp.bfloat16),
            (),
            *[pieces[s, p] for p in range(pairs)],
            *weights[3:],
            after=sections[:],
        )
        sections.append(section)
        halos.append(lax.ppermute(section, "rows", band_moves[s]))
    partials = kernel_call(
        inner_kernel,
        "inner",
        4_000_000_000,
        [jax.ShapeDtypeStruct(shape, jnp.float32)] * 2,
        (side_arg,),
        *sections,
        mlp_up,
        mix_kernel,
        mlp_down,
    )
    results, crossed, earlier = {}, {}, []
    calls = [(1, list(range(pairs))), (0, list(range(1, pairs))), (0, [0])]
    for s, chosen in calls:
        finished = kernel_call(
            functools.partial(outer_kernel, left, s, chosen),
            "outer",
            500_000_000 * len(chosen),
            jax.ShapeDtypeStruct((len(chosen),) + shape[1:], jnp.bfloat16),
            (side_arg, edge_args[1 - s]),
            partials[s],
            halos[1 - s],
            mlp_up,
            mix_kernel,
            mlp_down,
            after=earlier,
        )
        earlier = [finished]
        for place, p in enumerate(chosen):
            piece = finished[place, :, :cols]
            if (s, p) != (0, 0):
                back = [(j, i) for i, j in chip_moves(s, p)]
                piece = lax.ppermute(piece, both, back)
            results[s, p] = piece
    for group in (slots[:1] + slots[pairs:pairs + 1], slots[1:pairs] + slots[pairs + 1:]):
        sent = jnp.stack([results[slot][1] for slot in group])
        received = lax.ppermute(sent, "frame", siblings)
        for index, slot in enumerate(group):
            crossed[slot] = received[index]
    strips = [[], []]
    for owner in range(owners):
        own, other = results[slots[0]][0], crossed[slots[0]]
        for slot in slots[1:]:
            here = owner_at(*slot) == owner
            own = jnp.where(here, results[slot][0], own)
            other = jnp.where(here, crossed[slot], other)
        strips[0].append(jnp.where(frame % 2 == 0, own, other))
        strips[1].append(jnp.where(frame % 2 == 0, other, own))
    return jnp.stack([jnp.concatenate(strip) for strip in strips]).reshape(video.shape)


def solution(mesh):
    in_specs = (P(None, "frame", "rows", None, None), P(), P(), P(), P(), P(), P(), P(), P(), P())
    out_specs = P(None, "frame", "rows", None, None)
    return jax.shard_map(shards, mesh=mesh, in_specs=in_specs, out_specs=out_specs, check_vma=False)
```

```python
import functools

import jax
import jax.numpy as jnp
from jax import lax
from jax.experimental import pallas as pl
from jax.experimental.pallas import tpu as pltpu
from jax.sharding import PartitionSpec as P

HEADS = 8
HEAD_DIM = 32
SCALE_LOG2 = HEAD_DIM ** (-0.5) * 1.4426950408889634
VMEM_LIMIT = 40 * 1024 * 1024


def round_up(value, unit):
    return (value + unit - 1) // unit * unit


def layer_norm(widened):
    centred = widened - jnp.mean(widened, axis=-1, keepdims=True)
    variance = jnp.mean(centred * centred, axis=-1, keepdims=True)
    return (centred * lax.rsqrt(variance + 1e-05)).astype(jnp.bfloat16)


def dot_dims(lhs, rhs, lhs_dim, rhs_dim):
    return lax.dot_general(
        lhs, rhs, (((lhs_dim,), (rhs_dim,)), ((), ())), preferred_element_type=jnp.float32
    )


def stereo_rows(left, cols, rows, rows_other, qk_ref, v_ref, out_ref, windows_ref):
    width, channels = rows.shape
    normed = layer_norm(rows)
    normed_other = layer_norm(rows_other)
    queries = dot_dims(normed, qk_ref[:, :channels], 1, 0).astype(jnp.bfloat16)
    keys = dot_dims(normed_other, qk_ref[:, channels:], 1, 0).astype(jnp.bfloat16)
    values = dot_dims(normed_other, v_ref[...], 1, 0).astype(jnp.bfloat16)
    lane_head = lax.broadcasted_iota(jnp.int32, (width, 128), 1) // HEAD_DIM
    zero = jnp.zeros((), jnp.bfloat16)
    ones = jnp.ones((width, 128), jnp.bfloat16)
    owners, window, _ = windows_ref.shape
    tail = round_up((owners - 1) * cols + window, 8) - width
    per_group = 128 // HEAD_DIM

    def head_scores(head):
        lanes = slice(head // per_group * 128, head // per_group * 128 + 128)
        mask = lane_head == head % per_group
        return dot_dims(queries[:, lanes], jnp.where(mask, keys[:, lanes], zero), 1, 1)

    totals = [jnp.zeros((width, 128), jnp.float32) for _ in range(channels // 128)]
    ahead = [head_scores(head) for head in range(3)]
    for head in range(HEADS):
        if head + 3 < HEADS:
            ahead.append(head_scores(head + 3))
        scores = ahead.pop(0)
        group = head // per_group
        top = jnp.max(scores, axis=1, keepdims=True)
        weights = jnp.exp2((scores - top) * SCALE_LOG2).astype(jnp.bfloat16)
        mask = lane_head == head % per_group
        values_head = jnp.where(mask, values[:, group * 128 : group * 128 + 128], zero)
        mixed = dot_dims(weights, jnp.concatenate([values_head, ones], axis=1), 1, 0)
        totals[group] = totals[group] + mixed[:, :128] * (1.0 / mixed[:, 128:])
    groups = [total.astype(jnp.bfloat16) for total in totals]
    update = dot_dims(jnp.concatenate(groups, axis=1), out_ref[...], 1, 0)
    padded = jnp.concatenate([rows + update, jnp.zeros((tail, channels), jnp.float32)], axis=0)
    padded = pltpu.roll(padded, left, 0)
    for owner in range(owners):
        windows_ref[owner] = padded[owner * cols : owner * cols + window].astype(jnp.bfloat16)


def first_kernel(left, cols, core_ref, *refs):
    count = (len(refs) - 2) // 2
    sources, windows_ref = refs[:count], refs[count]
    targets, sems = (refs[-2], *refs[count + 1 : -2]), refs[-1]
    copies = [
        pltpu.make_async_copy(source, target, sems.at[index])
        for index, (source, target) in enumerate(zip(sources, targets))
    ]
    for copy in copies:
        copy.start()
    for copy in copies[:4]:
        copy.wait()
    second_kernel(left, cols, core_ref, *targets[:4], windows_ref)
    for copy in copies[4:]:
        copy.wait()


def second_kernel(left, cols, core_ref, video_ref, qk_ref, v_ref, out_ref, windows_ref):
    core = core_ref[0]
    width, channels = video_ref.shape[-2:]
    rows = video_ref[core].reshape(width, channels).astype(jnp.float32)
    rows_other = video_ref[1 - core].reshape(width, channels).astype(jnp.float32)
    stereo_rows(left, cols, rows, rows_other, qk_ref, v_ref, out_ref, windows_ref)


def first_stereo(core, video, owners, left, window, *weights):
    width, channels = video.shape[-2:]
    operands = [pltpu.with_memory_space_constraint(array, pltpu.HBM) for array in (video, *weights)]
    vmem = pl.BlockSpec(memory_space=pltpu.VMEM)
    return pl.pallas_call(
        functools.partial(first_kernel, left, width // owners),
        in_specs=[pl.BlockSpec(memory_space=pltpu.SMEM)]
        + [pl.BlockSpec(memory_space=pltpu.HBM)] * len(operands),
        out_specs=[vmem] * len(operands),
        out_shape=[jax.ShapeDtypeStruct((owners, window, channels), jnp.bfloat16)]
        + [jax.ShapeDtypeStruct(array.shape, array.dtype) for array in weights],
        scratch_shapes=[
            pltpu.VMEM(video.shape, video.dtype),
            pltpu.SemaphoreType.DMA((len(operands),)),
        ],
        compiler_params=pltpu.CompilerParams(vmem_limit_bytes=VMEM_LIMIT),
        cost_estimate=pl.CostEstimate(
            flops=2_400_000_000, bytes_accessed=2_000_000, transcendentals=2_000_000
        ),
        name="stereo",
    )(core, *operands)


def head_sum(product):
    channels, width = product.shape
    return jnp.sum(product.reshape(HEADS, HEAD_DIM, width), axis=1, keepdims=True)


def temporal_kernel(pairs, order, *refs):
    pieces, (qk_ref, v_ref, out_ref, section_ref) = refs[:pairs][::order], refs[pairs:]
    _, pair_size, window, channels = section_ref.shape
    frames = pairs * pair_size
    rows = jnp.concatenate(
        [piece[...].reshape(pair_size * window, channels) for piece in pieces], axis=0
    ).astype(jnp.float32)
    normed = layer_norm(rows)
    pairs_t = dot_dims(qk_ref[...], normed, 0, 1).astype(jnp.bfloat16)
    queries, keys = pairs_t[:channels], pairs_t[channels:]
    values = dot_dims(v_ref[...], normed, 0, 1).astype(jnp.bfloat16)
    attended = []
    for frame in range(frames):
        query = queries[:, frame * window : (frame + 1) * window].astype(jnp.float32)
        scores = [
            head_sum(query * keys[:, other * window : (other + 1) * window].astype(jnp.float32))
            for other in range(frames)
        ]
        top = functools.reduce(jnp.maximum, scores)
        weights = [jnp.exp2((score - top) * SCALE_LOG2) for score in scores]
        inverse = 1.0 / functools.reduce(jnp.add, weights)
        mixed = jnp.zeros((HEADS, HEAD_DIM, window), jnp.float32)
        for other in range(frames):
            value = values[:, other * window : (other + 1) * window].astype(jnp.float32)
            mixed = mixed + value.reshape(HEADS, HEAD_DIM, window) * (weights[other] * inverse)
        attended.append(mixed.reshape(channels, window).astype(jnp.bfloat16))
    update = dot_dims(jnp.concatenate(attended, axis=1), out_ref[...], 0, 0)
    section_ref[...] = (rows + update).astype(jnp.bfloat16).reshape(section_ref.shape)


def kernel_call(body, name, flops, out_shape, scalars, *operands, after=()):
    count = len(scalars) + len(operands)

    def ordered_body(*refs):
        body(*refs[:count], *refs[count + len(after) :])

    return pl.pallas_call(
        ordered_body,
        in_specs=[pl.BlockSpec(memory_space=pltpu.SMEM)] * len(scalars)
        + [pl.BlockSpec(memory_space=pltpu.VMEM)] * len(operands)
        + [pl.BlockSpec(memory_space=pl.ANY)] * len(after),
        out_specs=jax.tree.map(lambda _: pl.BlockSpec(memory_space=pltpu.VMEM), out_shape),
        out_shape=out_shape,
        compiler_params=pltpu.CompilerParams(vmem_limit_bytes=VMEM_LIMIT),
        cost_estimate=pl.CostEstimate(flops=flops, bytes_accessed=3_000_000, transcendentals=0),
        name=name,
    )(*scalars, *operands, *after)


def double_gelu(values):
    inner = values * (
        jnp.bfloat16(0.7978845608028654) + jnp.bfloat16(0.035677408136300125) * (values * values)
    )
    return values + values * jnp.tanh(inner)


def half_taps(mix_ref, tap, lanes):
    return mix_ref[tap, :, lanes] * jnp.bfloat16(0.5)


def mlp_mix(columns, window):
    columns = [column.astype(jnp.float32) for column in columns]
    return (
        pltpu.roll(columns[0], 1, 0) + columns[1] + pltpu.roll(columns[2], window - 1, 0)
    ).astype(jnp.bfloat16)


CHUNK = 256


def mlp_hidden(normed, up_ref, start):
    product = dot_dims(normed, up_ref[:, start : start + CHUNK], 1, 0)
    return double_gelu(product.astype(jnp.bfloat16))


def inner_kernel(side_ref, own_ref, next_ref, up_ref, mix_ref, down_ref, *partial_refs):
    pairs, pair_size, window, channels = own_ref.shape
    other_tap = (2 - 2 * side_ref[0], 2 * side_ref[0])
    for pair in range(pairs):
        for member in range(pair_size):
            rows = jnp.concatenate([own_ref[pair, member], next_ref[pair, member]], axis=0)
            rows = rows.astype(jnp.float32)
            normed = layer_norm(rows)
            total = rows
            for start in range(0, up_ref.shape[1], CHUNK):
                lanes = slice(start, start + CHUNK)
                hidden = mlp_hidden(normed, up_ref, start)
                lines = [hidden[:window], hidden[window:]]
                same = half_taps(mix_ref, 1, lanes)
                mixed = []
                for slot in range(2):
                    across = half_taps(mix_ref, other_tap[slot], lanes)
                    mixed.append(
                        mlp_mix(
                            [
                                lines[slot] * same[b][None] + lines[1 - slot] * across[b][None]
                                for b in range(3)
                            ],
                            window,
                        )
                    )
                total = total + dot_dims(jnp.concatenate(mixed, axis=0), down_ref[lanes], 1, 0)
            for slot in range(2):
                partial_refs[slot][pair, member] = total[slot * window : (slot + 1) * window]


def outer_kernel(
    left, slot, chosen, side_ref, edge_ref, partial_ref, halo_ref, up_ref, mix_ref, down_ref, out_ref
):
    _, pair_size, window, channels = partial_ref.shape
    tap = 2 * side_ref[0] if slot == 0 else 2 - 2 * side_ref[0]
    for place, pair in enumerate(chosen):
        rows = halo_ref[pair].reshape(pair_size * window, channels).astype(jnp.float32)
        normed = layer_norm(jnp.where(edge_ref[0] == 1, jnp.zeros_like(rows), rows))
        total = partial_ref[pair].reshape(pair_size * window, channels)
        for start in range(0, up_ref.shape[1], CHUNK):
            lanes = slice(start, start + CHUNK)
            hidden = mlp_hidden(normed, up_ref, start)
            across = half_taps(mix_ref, tap, lanes)
            mixed = [
                mlp_mix(
                    [
                        hidden[member * window : (member + 1) * window] * across[b][None]
                        for b in range(3)
                    ],
                    window,
                )
                for member in range(pair_size)
            ]
            total = total + dot_dims(jnp.concatenate(mixed, axis=0), down_ref[lanes], 1, 0)
        for member in range(pair_size):
            shifted = pltpu.roll(total[member * window : (member + 1) * window], window - left, 0)
            out_ref[place, member] = shifted.astype(jnp.bfloat16)


def shards(
    video,
    stereo_qk,
    stereo_v,
    stereo_out,
    temporal_qk,
    temporal_v,
    temporal_out,
    mlp_up,
    mix_kernel,
    mlp_down,
):
    width, channels = video.shape[-2:]
    frame_size, rows_size = lax.axis_size("frame"), lax.axis_size("rows")
    pairs = frame_size // 2
    owners = frame_size
    cols = width // owners
    window = round_up(cols + 2, 16)
    left = (window - cols) // 2
    frame, row = lax.axis_index("frame"), lax.axis_index("rows")
    pair, side = frame // 2, row % 2
    side_arg = side.astype(jnp.int32)[None]
    both = ("frame", "rows")
    slots = [(s, p) for s in range(2) for p in range(pairs)]

    def owner_at(s, p):
        return lax.rem(pair + p, pairs) * 2 + (side ^ s)

    def chip_moves(s, p):
        return [
            (
                f * rows_size + r,
                ((f // 2 + p) % pairs * 2 + f % 2) * rows_size + (r ^ s),
            )
            for f in range(frame_size)
            for r in range(rows_size)
        ]

    siblings = [(f, f ^ 1) for f in range(frame_size)]
    bands = rows_size // 2
    band_moves = []
    for slot in range(2):
        moves = []
        for r in range(rows_size):
            band = r // 2 + (1 if (r + slot) % 2 else -1)
            moves.append((r, band * 2 + r % 2 if 0 <= band < bands else r ^ 1))
        band_moves.append(moves)
    first_band, last_band = row // 2 == 0, row // 2 == bands - 1
    at_edge = (
        jnp.where(side == 0, last_band, first_band),
        jnp.where(side == 0, first_band, last_band),
    )
    edge_args = [edge.astype(jnp.int32)[None] for edge in at_edge]
    core_arg = (frame % 2).astype(jnp.int32)[None]
    sibling_video = lax.ppermute(video, "frame", siblings)
    windows, *weights = first_stereo(
        core_arg,
        video,
        owners,
        left,
        window,
        stereo_qk,
        stereo_v,
        stereo_out,
        temporal_qk,
        temporal_v,
        temporal_out,
    )
    sibling_windows = kernel_call(
        functools.partial(second_kernel, left, cols),
        "stereo",
        2_400_000_000,
        jax.ShapeDtypeStruct(windows.shape, windows.dtype),
        (core_arg,),
        sibling_video,
        *weights[:3],
    )
    pieces = {}
    for s, p in slots:
        index = owner_at(s, p)
        piece = jnp.stack(
            [
                lax.dynamic_index_in_dim(array, index, 0, keepdims=False)
                for array in (windows, sibling_windows)
            ]
        )
        if (s, p) != (0, 0):
            piece = lax.ppermute(piece, both, chip_moves(s, p))
        pieces[s, p] = piece
    shape = (pairs, 2, window, channels)
    sections, halos = [], []
    for s in range(2):
        section = kernel_call(
            functools.partial(temporal_kernel, pairs, 1),
            "temporal",
            1_000_000_000,
            jax.ShapeDtypeStruct(shape, jnp.bfloat16),
            (),
            *[pieces[s, p] for p in range(pairs)],
            *weights[3:],
            after=sections[:],
        )
        sections.append(section)
        halos.append(lax.ppermute(section, "rows", band_moves[s]))
    partials = kernel_call(
        inner_kernel,
        "inner",
        4_000_000_000,
        [jax.ShapeDtypeStruct(shape, jnp.float32)] * 2,
        (side_arg,),
        *sections,
        mlp_up,
        mix_kernel,
        mlp_down,
    )
    results, crossed, earlier = {}, {}, []
    calls = [(1, list(range(pairs))), (0, list(range(1, pairs))), (0, [0])]
    for s, chosen in calls:
        finished = kernel_call(
            functools.partial(outer_kernel, left, s, chosen),
            "outer",
            500_000_000 * len(chosen),
            jax.ShapeDtypeStruct((len(chosen),) + shape[1:], jnp.bfloat16),
            (side_arg, edge_args[1 - s]),
            partials[s],
            halos[1 - s],
            mlp_up,
            mix_kernel,
            mlp_down,
            after=earlier,
        )
        earlier = [finished]
        for place, p in enumerate(chosen):
            piece = finished[place, :, :cols]
            if (s, p) != (0, 0):
                back = [(j, i) for i, j in chip_moves(s, p)]
                piece = lax.ppermute(piece, both, back)
            results[s, p] = piece
    for group in (slots[:1] + slots[pairs:pairs + 1], slots[1:pairs] + slots[pairs + 1:]):
        sent = jnp.stack([results[slot][1] for slot in group])
        received = lax.ppermute(sent, "frame", siblings)
        for index, slot in enumerate(group):
            crossed[slot] = received[index]
    strips = [[], []]
    for owner in range(owners):
        own, other = results[slots[0]][0], crossed[slots[0]]
        for slot in slots[1:]:
            here = owner_at(*slot) == owner
            own = jnp.where(here, results[slot][0], own)
            other = jnp.where(here, crossed[slot], other)
        strips[0].append(jnp.where(frame % 2 == 0, own, other))
        strips[1].append(jnp.where(frame % 2 == 0, other, own))
    return jnp.stack([jnp.concatenate(strip) for strip in strips]).reshape(video.shape)


def solution(mesh):
    in_specs = (P(None, "frame", "rows", None, None), P(), P(), P(), P(), P(), P(), P(), P(), P())
    out_specs = P(None, "frame", "rows", None, None)
    return jax.shard_map(shards, mesh=mesh, in_specs=in_specs, out_specs=out_specs, check_vma=False)
```
